512 devices in a mesh: recv: 128 (over z, x, core), src: 4 (over y).
Axes of the slice: x: 4, y: 4, z: 16, core: 2. Of those that a mesh axis runs over, the one named last changes fastest.
Arguments:
- interactions: int32 [3, 49152], P(None, ('recv', 'src')), may hold values from 0 to 4095, as said below
- list_lengths: int32 [512], P(('recv', 'src')), may hold values from 48 to 96, as said below
- kernels: float32 [2048, 128, 16, 128], P(('recv', 'src')), may hold values from -0.0210316469 to 0.0210316469
- prestress: float32 [4096, 128], P(('recv', 'src')), may hold values from 2 to 3
- friction: float32 [4096, 128], P(('recv', 'src')), may hold values from 0.2 to 0.5
- load_rate: float32 [4096, 128], P(('recv', 'src')), may hold values from 0.04 to 0.08
Outputs:
- slip_rates: float32 [4096, 96, 128], P(('recv', 'src'))
The draws below stay inside these ranges and needn't reach their ends.
Inputs may be any that keep to these rules, and one draw needn't show every extreme that they name: `interactions`: column e belongs to device block g = e // 96, g = i * 4 + j. Its receiver patch lies in [i * 4 * 8, (i + 1) * 4 * 8); its source patch p satisfies (p // 8) mod 4 == j; its owner is p // 32; its lag offset lies in [32, 48]. The entries of one block name at most 1 distinct source patches of one owner, and in every draw some owner supplies exactly that many distinct source patches to every block. `list_lengths`: some device's list is full and some device's list holds exactly half, in every draw.
All inputs are finite; a program needn't handle non-finite values.
Results may differ from the reference program's by a relative error of at most 0.0003.
Values sent between devices are 32-bit elements; how exact they have to be, the bound alone decides.
A program may use at most 128 MiB of HBM per device.

```python
import math
import jax
import jax.numpy as jnp
from jax import lax

PE = 128
LAGS = 16
BLOCK = 32
BLOCKS = 3
NEWTON = 4
PATCH_DEV = 8
KER_DEV = 4
ENT_KER = 24
ENT_DEV = 96
PEER_CAP = 1
OWNERS = 128
STRIPS = 4
PATCHES = 4096
KERNEL_TOTAL = 2048


def draw_interactions(key, part):
    devices = OWNERS * STRIPS
    key_recv, key_src, key_lag, key_hot, key_weight, key_score, key_order = jax.random.split(jax.random.fold_in(key, 11), 7)
    device_ids = jnp.arange(devices, dtype=jnp.int32)
    group_idx = device_ids // STRIPS
    strip_idx = device_ids % STRIPS
    receivers = group_idx[:, None] * (STRIPS * PATCH_DEV) + jax.random.randint(key_recv, (devices, ENT_DEV), 0, STRIPS * PATCH_DEV)
    slot_count = OWNERS * PEER_CAP
    slot_ids = jnp.arange(slot_count, dtype=jnp.int32)
    slot_owner = slot_ids // PEER_CAP
    slot_rank = slot_ids % PEER_CAP
    starting_patch = jax.random.randint(key_src, (devices, OWNERS), 0, PATCH_DEV)
    slot_local = (starting_patch[:, slot_owner] + slot_rank[None, :]) % PATCH_DEV
    slot_patch = (slot_owner[None, :] * STRIPS + strip_idx[:, None]) * PATCH_DEV + slot_local
    hot_owner = jax.random.randint(key_hot, (), 0, OWNERS)
    owner_weight = jax.random.randint(key_weight, (OWNERS,), 1, 5)
    owner_weight = jnp.where(jnp.arange(OWNERS, dtype=jnp.int32) == hot_owner, 16, owner_weight)
    cumulative = jnp.cumsum(owner_weight[slot_owner])
    total_weight = cumulative[-1]
    picks = jax.random.randint(key_score, (devices, ENT_DEV), 0, 2 ** 30) % total_weight
    chosen = jnp.sum((cumulative[None, None, :] <= picks[:, :, None]).astype(jnp.int32), axis=2)
    forced = hot_owner * PEER_CAP + jnp.arange(PEER_CAP, dtype=jnp.int32)
    chosen = chosen.at[:, :PEER_CAP].set(jnp.broadcast_to(forced[None, :], (devices, PEER_CAP)))
    order_keys = jax.random.split(key_order, devices)
    chosen = jax.vmap(jax.random.permutation)(order_keys, chosen)
    sources = jnp.take_along_axis(slot_patch, chosen, axis=1)
    delays = jax.random.randint(key_lag, (devices, ENT_DEV), BLOCK, 2 * BLOCK - LAGS + 1)
    return jnp.stack([receivers.reshape(-1), sources.reshape(-1), delays.reshape(-1)]).astype(jnp.int32)


def draw_list_lengths(key, part):
    devices = OWNERS * STRIPS
    key_len, key_perm = jax.random.split(jax.random.fold_in(key, 23), 2)
    lengths = jax.random.randint(key_len, (devices,), ENT_DEV // 2, ENT_DEV + 1)
    shuffled = jax.random.permutation(key_perm, devices)
    lengths = lengths.at[shuffled[0]].set(ENT_DEV).at[shuffled[1]].set(ENT_DEV // 2)
    return lengths.astype(jnp.int32)


def draw_kernels(key, part):
    key_base, key_gain = jax.random.split(jax.random.fold_in(key, 37), 2)
    full_shape = (KERNEL_TOTAL, PE, LAGS, PE)
    spread = float(8 * LAGS * PE * ENT_DEV // PATCH_DEV) ** (-0.5)
    base = jnp.clip(jax.random.normal(key_base, full_shape, jnp.float32), -6.0, 6.0) * spread
    gains = jax.random.uniform(key_gain, (KERNEL_TOTAL, PE, 1, PE), jnp.float32, 0.5, 1.5)
    centred = jnp.arange(LAGS, dtype=jnp.float32) - 0.5 * (LAGS - 1)
    bend = centred * centred
    bend = bend - jnp.mean(bend)
    bend = bend / jnp.max(jnp.abs(bend))
    fourth = jnp.sum(centred ** 4) / jnp.sum(centred ** 2)
    twist = centred ** 3 - fourth * centred
    twist = twist / jnp.max(jnp.abs(twist))
    profile = 0.002 * bend + 0.003 * twist
    return base + gains * profile[None, None, :, None]


def shard_levels(own_key, extent, cuts, least, top_value):
    factor_of = 1.0
    for position, parts in cuts:
        steps = jax.random.uniform(jax.random.fold_in(jax.random.fold_in(own_key, 6), position), (parts,), jnp.float32, least / len(cuts), top_value / len(cuts))
        factor_of = factor_of * jnp.repeat(jnp.exp(steps), extent[position] // parts).reshape((-1,) + (1,) * (len(extent) - 1 - position))
    return factor_of


def setup_inputs(seed: int = 0) -> dict:
    splits = jax.random.split(jax.random.key(seed), 7)
    return {
        "interactions": draw_interactions(jax.random.fold_in(splits[6], 71), 0),
        "list_lengths": draw_list_lengths(jax.random.fold_in(splits[6], 71), 0),
        "kernels": draw_kernels(jax.random.fold_in(splits[6], 71), 0),
        "prestress": jnp.clip(2.0 + 1.0 * jax.random.uniform(splits[3], (PATCHES, PE), jnp.float32) ** shard_levels(splits[3], (PATCHES, PE), ((0, 512),), -0.2, 0.2), 2.0, 3.0),
        "friction": jnp.clip(jnp.exp(math.log(0.5) - 0.9162907 * jax.random.uniform(splits[4], (PATCHES, PE), jnp.float32) ** shard_levels(splits[4], (PATCHES, PE), ((0, 512),), -0.2, 0.2)), 0.2, 0.5),
        "load_rate": jnp.clip(jnp.exp(math.log(0.08) - 0.6931472 * jax.random.uniform(splits[5], (PATCHES, PE), jnp.float32) ** shard_levels(splits[5], (PATCHES, PE), ((0, 512),), -0.2, 0.2)), 0.04, 0.08),
    }


damping = 0.5

def inverse_sinh(values):
    magnitude = jnp.abs(values)
    result = jnp.log(magnitude + jnp.sqrt(1.0 + magnitude * magnitude))
    return jnp.where(values < 0, -result, result)

def friction_solve(drive, friction):
    rates = jnp.zeros_like(drive)
    for newton_step in range(NEWTON):
        misfit = damping * rates + friction * inverse_sinh(rates) - drive
        slope_now = damping + friction * lax.rsqrt(1.0 + rates * rates)
        rates = rates - misfit / slope_now
    return rates

def lagged_stack(windows, delays):

    def cut_window(window, delay):
        return lax.dynamic_slice_in_dim(window, 2 * BLOCK - delay - (LAGS - 1), BLOCK + LAGS - 1, 0)
    segments = jax.vmap(cut_window)(windows, delays)
    pieces = [segments[:, LAGS - 1 - lag_idx:LAGS - 1 - lag_idx + BLOCK] for lag_idx in range(LAGS)]
    return jnp.stack(pieces, axis=2)

def interaction_stress(window_all, interactions, list_lengths, kernels):

    def one_device(total, device):
        entries = lax.dynamic_slice_in_dim(interactions, device * ENT_DEV, ENT_DEV, 1)
        windows = jnp.take(window_all, entries[1], axis=0)
        stacked_rows = lagged_stack(windows, entries[2]).reshape(KER_DEV, ENT_KER * BLOCK, LAGS * PE)
        kernel_matrices = lax.dynamic_slice_in_dim(kernels, device * KER_DEV, KER_DEV, 0).reshape(KER_DEV, PE, LAGS * PE)
        stress_terms = jnp.einsum('svf,sif->svi', stacked_rows, kernel_matrices, precision=lax.Precision.HIGHEST)
        stress_terms = stress_terms.reshape(ENT_DEV, BLOCK, PE)
        live = (jnp.arange(ENT_DEV, dtype=jnp.int32) < list_lengths[device]).astype(jnp.float32)
        return (total.at[entries[0]].add(stress_terms * live[:, None, None]), None)
    start = jnp.zeros((PATCHES, BLOCK, PE), jnp.float32)
    total, unused = lax.scan(one_device, start, jnp.arange(OWNERS * STRIPS, dtype=jnp.int32))
    return total

def reference(interactions, list_lengths, kernels, prestress, friction, load_rate):
    zeros_front = jnp.zeros((PATCHES, 2 * BLOCK, PE), jnp.float32)
    finished_blocks = []
    for block_idx in range(BLOCKS):
        if block_idx == 0:
            stress = jnp.zeros((PATCHES, BLOCK, PE), jnp.float32)
        else:
            padded = jnp.concatenate([zeros_front] + finished_blocks, axis=1)
            window_all = padded[:, block_idx * BLOCK:block_idx * BLOCK + 2 * BLOCK]
            stress = interaction_stress(window_all, interactions, list_lengths, kernels)
        times = (block_idx * BLOCK + 1 + jnp.arange(BLOCK, dtype=jnp.int32)).astype(jnp.float32)
        drive = prestress[:, None, :] + load_rate[:, None, :] * times[None, :, None] + stress
        finished_blocks.append(friction_solve(drive, friction[:, None, :]))
    return jnp.concatenate(finished_blocks, axis=1)
```

```python
import functools

import jax
import jax.numpy as jnp
from jax import lax
from jax.experimental import pallas as pl
from jax.experimental.pallas import tpu as pltpu
from jax.sharding import PartitionSpec as P

MESH = pl.DeviceIdType.MESH
F32 = jnp.float32
BF16 = jnp.bfloat16

PE = 128
LAGS = 16
BLOCK = 32
PATCH = 8
KER = 4
ENT = 24
NENT = KER * ENT
GRP = 8
SRC = 4
DAMP = 0.5
VMEM_LIMIT = 56 * 1024 * 1024
PAD = 6


def newton(drive, friction):
    v = drive / (DAMP + friction)
    for _ in range(3):
        square = 1.0 + v * v
        root = lax.rsqrt(square)
        mag = jnp.log(jnp.abs(v) + square * root)
        arc = jnp.where(v < 0, -mag, mag)
        slope = DAMP + friction * root
        v = v - (DAMP * v + friction * arc - drive) / slope
    return v


def split(value):
    high = value.astype(BF16)
    return high, (value - high.astype(F32)).astype(BF16)


def ask_kernel(
    n_z, inter_ref, pre_ref, fri_ref, load_ref, kern_ref,
    table_ref, weight_ref, wanted_ref,
    zbuf, req, asked, picked, kern_f32, req_s, req_r, z_s, z_r, x_s, x_r, loc,
):
    me, y = lax.axis_index("recv"), lax.axis_index("src")
    z, k_me = me // GRP, me % GRP
    barrier = pltpu.get_barrier_semaphore()
    for dz in range(1, n_z):
        pl.semaphore_signal(barrier, inc=1, device_id=(((z + dz) % n_z) * GRP + k_me, y), device_id_type=MESH)
    for dk in range(1, GRP):
        pl.semaphore_signal(barrier, inc=1, device_id=(z * GRP + (k_me + dk) % GRP, y), device_id_type=MESH)
    fetch = pltpu.make_async_copy(kern_ref, kern_f32, loc.at[0])
    fetch.start()
    zbuf[z, 0:8, :] = pre_ref[...]
    zbuf[z, 8:16, :] = fri_ref[...]
    zbuf[z, 16:24, :] = load_ref[...]
    row = inter_ref[1:2, :]
    eye = lax.broadcasted_iota(jnp.int32, (NENT, NENT), 0) == lax.broadcasted_iota(jnp.int32, (NENT, NENT), 1)
    column = jnp.sum(jnp.where(eye, jnp.broadcast_to(row, (NENT, NENT)), 0), axis=1, keepdims=True)
    owner = lax.shift_right_logical(column, 5)
    place = jnp.bitwise_and(column, PATCH - 1)
    hit = owner == lax.broadcasted_iota(jnp.int32, (NENT, n_z * GRP), 1)
    wanted = jnp.max(jnp.where(hit, place, 0), axis=0, keepdims=True)
    req[k_me] = jnp.broadcast_to(wanted, (8, n_z * GRP))
    pl.semaphore_wait(barrier, n_z - 1 + GRP - 1)
    sends = []
    for dk in range(1, GRP):
        sends.append(
            pltpu.make_async_remote_copy(
                src_ref=req.at[k_me], dst_ref=req.at[k_me], send_sem=req_s.at[dk - 1], recv_sem=req_r.at[dk - 1],
                device_id=(z * GRP + (k_me + dk) % GRP, y), device_id_type=MESH,
            )
        )
        sends[-1].start()
    zsends = []
    order = sorted(range(1, n_z), key=lambda d: -min(d, n_z - d))
    for dz in order:
        zsends.append(
            pltpu.make_async_remote_copy(
                src_ref=zbuf.at[z], dst_ref=zbuf.at[z], send_sem=z_s.at[dz - 1], recv_sem=z_r.at[dz - 1],
                device_id=(((z + dz) % n_z) * GRP + k_me, y), device_id_type=MESH,
            )
        )
        zsends[-1].start()
    for copy in sends:
        copy.wait()
    down = pltpu.make_async_copy(req, asked, loc.at[1])
    down.start()
    down.wait()
    for copy in zsends:
        copy.wait()

    def pick(k, carry):
        for zz in range(n_z):
            p = asked[k, 0, zz * GRP + k_me]
            for i in range(3):
                picked[k, i, zz : zz + 1, :] = zbuf[zz, pl.ds(8 * i + p, 1), :]
        return carry

    lax.fori_loop(0, GRP, pick, 0)
    xsends = []
    for dk in range(1, GRP):
        k = (k_me + dk) % GRP
        xsends.append(
            pltpu.make_async_remote_copy(
                src_ref=picked.at[k], dst_ref=table_ref.at[k_me], send_sem=x_s.at[dk - 1], recv_sem=x_r.at[dk - 1],
                device_id=(z * GRP + k, y), device_id_type=MESH,
            )
        )
        xsends[-1].start()
    table_ref[k_me] = picked[k_me]
    wanted_ref[...] = req[...]
    fetch.wait()

    def weights(i, carry):
        k, lag = i // LAGS, i % LAGS
        part = kern_f32[k, pl.ds(lag, PE, stride=LAGS), :]
        high, low = split(part.T)
        at = pl.ds(pl.multiple_of(lag * PE, PE), PE)
        weight_ref[k, at, 0:PE] = high
        weight_ref[k, at, PE : 2 * PE] = low
        return carry

    lax.fori_loop(0, KER * LAGS, weights, 0)
    for copy in xsends:
        copy.wait()


def ask(n_z, interactions, prestress, friction, load_rate, kernels):
    vm = pl.BlockSpec(memory_space=pltpu.VMEM)
    owners = n_z * GRP
    return pl.pallas_call(
        functools.partial(ask_kernel, n_z),
        out_shape=(
            jax.ShapeDtypeStruct((GRP, 3, n_z, PE), F32),
            jax.ShapeDtypeStruct((KER, LAGS * PE, 2 * PE), BF16),
            jax.ShapeDtypeStruct((GRP, 8, owners), jnp.int32),
        ),
        in_specs=[vm, vm, vm, vm, pl.BlockSpec(memory_space=pl.ANY)],
        out_specs=(vm, vm, vm),
        scratch_shapes=[
            pltpu.VMEM((n_z, 24, PE), F32),
            pltpu.VMEM((GRP, 8, owners), jnp.int32),
            pltpu.SMEM((GRP, 8, owners), jnp.int32),
            pltpu.VMEM((GRP, 3, n_z, PE), F32),
            pltpu.VMEM((KER, LAGS * PE, PE), F32),
            pltpu.SemaphoreType.DMA((GRP - 1,)),
            pltpu.SemaphoreType.DMA((GRP - 1,)),
            pltpu.SemaphoreType.DMA((n_z - 1,)),
            pltpu.SemaphoreType.DMA((n_z - 1,)),
            pltpu.SemaphoreType.DMA((GRP - 1,)),
            pltpu.SemaphoreType.DMA((GRP - 1,)),
            pltpu.SemaphoreType.DMA((2,)),
        ],
        compiler_params=pltpu.CompilerParams(
            collective_id=0, has_side_effects=True, vmem_limit_bytes=VMEM_LIMIT
        ),
        name="ask",
    )(interactions, prestress, friction, load_rate, kernels)


def put(high_ref, low_ref, start, left, right):
    at = pl.ds(pl.multiple_of(start, 2 * ENT), 2 * ENT)
    high_ref[at, 0:PE], low_ref[at, 0:PE] = split(left)
    high_ref[at, PE : 2 * PE], low_ref[at, PE : 2 * PE] = split(right)


def conv_tile(k, start_rows, pairs, high_ref, low_ref, weight_ref, rows):
    wide = len(pairs) * 2 * PE
    high = jnp.concatenate([high_ref[pl.ds(s, rows), :] for s in start_rows], axis=1)
    low = jnp.concatenate([low_ref[pl.ds(s, rows), :] for s in start_rows], axis=1)
    weight = weight_ref[k, 0:wide, :]
    both = jnp.dot(high, weight, preferred_element_type=F32)
    rest = jnp.dot(low, weight[:, 0:PE], preferred_element_type=F32)
    return both[:, 0:PE] + both[:, PE : 2 * PE] + rest


def route(k, inter_ref, length_ref, group_base, terms, sum_ref):
    live = jnp.clip(length_ref[0] - k * ENT, 0, ENT)

    def add(e, carry):
        q = inter_ref[0, k * ENT + e] - group_base
        sum_ref[q] += terms[pl.ds(e, BLOCK, stride=ENT), :]
        return carry

    lax.fori_loop(0, live, add, 0)


def first_kernel(
    n_z, inter_ref, length_ref, base_ref, table_ref, weight_ref, sum_ref, early_ref,
    rows, high, low, terms,
):
    sum_ref[...] = jnp.zeros_like(sum_ref)
    high[0 : PAD * ENT, :] = jnp.zeros((PAD * ENT, 2 * PE), BF16)
    low[0 : PAD * ENT, :] = jnp.zeros((PAD * ENT, 2 * PE), BF16)

    for k in range(KER):

        def fill(e, carry):
            p = inter_ref[1, k * ENT + e]
            owner = lax.shift_right_logical(p, 5)
            zz, kk = owner // GRP, owner % GRP
            for i in range(3):
                rows[i, pl.ds(e, 1), :] = table_ref[kk, i, pl.ds(zz, 1), :]
            delay = inter_ref[2, k * ENT + e]
            rows[3, pl.ds(e, 1), :] = jnp.full((1, PE), delay, jnp.int32).astype(F32)
            return carry

        lax.fori_loop(0, ENT, fill, 0)
        pre, fri, load, delay = rows[0], rows[1], rows[2], rows[3]

        def history(u):
            time = lax.convert_element_type(u + 17, F32) - delay
            v = newton(pre + load * (time + 1.0), fri)
            return jnp.where((time >= 0.0) & (time < 32.0), v, 0.0)

        def pair(keep, i, before):
            now, after = history(15 + 2 * i), history(16 + 2 * i)
            left = jnp.concatenate([now, after], axis=0)
            put(high, low, (PAD + 2 * i) * ENT, left, jnp.concatenate([before, now], axis=0))
            if keep:
                early_ref[k, pl.ds(pl.multiple_of((2 * i - 16) * ENT, 2 * ENT), 2 * ENT), :] = left
            return after

        last = lax.fori_loop(0, 8, functools.partial(pair, False), jnp.zeros((ENT, PE), F32))
        lax.fori_loop(8, 16, functools.partial(pair, True), last)

        def more(i, carry):
            both = jnp.concatenate([history(47 + 2 * i), history(48 + 2 * i)], axis=0)
            early_ref[k, pl.ds(pl.multiple_of((2 * i + 16) * ENT, 2 * ENT), 2 * ENT), :] = both
            return carry

        lax.fori_loop(0, 8, more, 0)

        for m in range(4):
            pairs = [j for j in range(8) if 2 * j <= 8 * m + 7]
            starts = [(8 * m - 2 * j + PAD) * ENT for j in pairs]
            terms[8 * m * ENT : (8 * m + 8) * ENT, :] = conv_tile(k, starts, pairs, high, low, weight_ref, 8 * ENT)
        route(k, inter_ref, length_ref, base_ref[0], terms, sum_ref)


def first(n_z, interactions, lengths, base, table, weight):
    vm = pl.BlockSpec(memory_space=pltpu.VMEM)
    sm = pl.BlockSpec(memory_space=pltpu.SMEM)
    return pl.pallas_call(
        functools.partial(first_kernel, n_z),
        out_shape=(
            jax.ShapeDtypeStruct((SRC * PATCH, BLOCK, PE), F32),
            jax.ShapeDtypeStruct((KER, 32 * ENT, PE), F32),
        ),
        in_specs=[sm, sm, sm, vm, vm],
        out_specs=(vm, vm),
        scratch_shapes=[
            pltpu.VMEM((4, ENT, PE), F32),
            pltpu.VMEM(((PAD + 32) * ENT, 2 * PE), BF16),
            pltpu.VMEM(((PAD + 32) * ENT, 2 * PE), BF16),
            pltpu.VMEM((BLOCK * ENT, PE), F32),
        ],
        compiler_params=pltpu.CompilerParams(vmem_limit_bytes=VMEM_LIMIT),
        name="first",
    )(interactions, lengths, base, table, weight)


def second_kernel(
    n_z, inter_ref, length_ref, base_ref, got_ref, weight_ref, early_ref, sum_ref,
    line, high, low, terms,
):
    sum_ref[...] = jnp.zeros_like(sum_ref)
    for k in range(KER):
        line[0 : 32 * ENT, :] = early_ref[k]
        line[32 * ENT : 48 * ENT, :] = jnp.zeros((16 * ENT, PE), F32)

        def place(e, carry):
            owner = lax.shift_right_logical(inter_ref[1, k * ENT + e], 5)
            delay = inter_ref[2, k * ENT + e]
            line[pl.ds((delay - 16) * ENT + e, BLOCK, stride=ENT), :] = got_ref[owner % GRP, owner // GRP]
            return carry

        lax.fori_loop(0, ENT, place, 0)

        def pair(i, carry):
            left = line[pl.ds(pl.multiple_of((2 * i + 2) * ENT, 2 * ENT), 2 * ENT), :]
            right = line[pl.ds(pl.multiple_of((2 * i + 1) * ENT, ENT), 2 * ENT), :]
            put(high, low, 2 * i * ENT, left, right)
            return carry

        lax.fori_loop(0, 23, pair, 0)
        for m in range(4):
            pairs = list(range(8))
            starts = [(8 * m + 14 - 2 * j) * ENT for j in pairs]
            terms[8 * m * ENT : (8 * m + 8) * ENT, :] = conv_tile(k, starts, pairs, high, low, weight_ref, 8 * ENT)
        route(k, inter_ref, length_ref, base_ref[0], terms, sum_ref)


def second(n_z, interactions, lengths, base, got, weight, early):
    vm = pl.BlockSpec(memory_space=pltpu.VMEM)
    sm = pl.BlockSpec(memory_space=pltpu.SMEM)
    return pl.pallas_call(
        functools.partial(second_kernel, n_z),
        out_shape=jax.ShapeDtypeStruct((SRC * PATCH, BLOCK, PE), F32),
        in_specs=[sm, sm, sm, vm, vm, vm],
        out_specs=vm,
        scratch_shapes=[
            pltpu.VMEM((64 * ENT, PE), F32),
            pltpu.VMEM((46 * ENT, 2 * PE), BF16),
            pltpu.VMEM((46 * ENT, 2 * PE), BF16),
            pltpu.VMEM((BLOCK * ENT, PE), F32),
        ],
        compiler_params=pltpu.CompilerParams(vmem_limit_bytes=VMEM_LIMIT),
        name="second",
    )(interactions, lengths, base, got, weight, early)


def start_strips(part_ref, parts, y_s, y_r):
    me, y = lax.axis_index("recv"), lax.axis_index("src")
    copies = []
    for dy in (2, 1, 3):
        to = (y + dy) % SRC
        copies.append(
            pltpu.make_async_remote_copy(
                src_ref=part_ref.at[pl.ds(to * PATCH, PATCH)], dst_ref=parts.at[dy - 1],
                send_sem=y_s.at[dy - 1], recv_sem=y_r.at[dy - 1],
                device_id=(me, to), device_id_type=MESH,
            )
        )
        copies[-1].start()
    return copies


def solve_patch(p, block, stress, pre_ref, fri_ref, load_ref):
    pre, fri, load = pre_ref[pl.ds(p, 1), :], fri_ref[pl.ds(p, 1), :], load_ref[pl.ds(p, 1), :]
    times = lax.broadcasted_iota(jnp.int32, (BLOCK, PE), 0).astype(F32) + float(block * BLOCK + 1)
    drive = pre + load * times
    if stress is not None:
        drive = drive + stress
    return newton(drive, jnp.broadcast_to(fri, (BLOCK, PE)))


def spread_kernel(
    n_z, part_ref, pre_ref, fri_ref, load_ref, asked, got_ref, rate_ref, *scratch
):
    half = n_z // 2
    parts, own, picked = scratch[:3]
    right = dict(enumerate(scratch[3 : 3 + half - 1], 1))
    left = dict(enumerate(scratch[3 + half - 1 : 3 + 2 * (half - 1)], 1))
    far = scratch[1 + 2 * half]
    y_s, y_r, r_s, r_r, l_s, l_r, x_s, x_r = scratch[2 + 2 * half :]
    right[half] = left[half] = far
    me, y = lax.axis_index("recv"), lax.axis_index("src")
    z, k_me = me // GRP, me % GRP
    to_right = (((z + 1) % n_z) * GRP + k_me, y)
    to_left = (((z + n_z - 1) % n_z) * GRP + k_me, y)
    barrier = pltpu.get_barrier_semaphore()
    for dy in range(1, SRC):
        pl.semaphore_signal(barrier, inc=1, device_id=(me, (y + dy) % SRC), device_id_type=MESH)
    for to in (to_right, to_left):
        pl.semaphore_signal(barrier, inc=1, device_id=to, device_id_type=MESH)
    for dk in range(1, GRP):
        pl.semaphore_signal(barrier, inc=1, device_id=(z * GRP + (k_me + dk) % GRP, y), device_id_type=MESH)
    pl.semaphore_wait(barrier, SRC - 1 + 2 + GRP - 1)

    strips = start_strips(part_ref, parts, y_s, y_r)
    for copy in strips:
        copy.wait_recv()

    def solve(p, carry):
        stress = part_ref[y * PATCH + p] + parts[0, p] + parts[1, p] + parts[2, p]
        v = solve_patch(p, 1, stress, pre_ref, fri_ref, load_ref)
        own[p] = v
        rate_ref[p] = v
        return carry

    lax.fori_loop(0, PATCH, solve, 0)

    def hop(source, target, h, s, send, recv, to):
        rows = pl.ds(h * (PATCH // 2), PATCH // 2)
        return pltpu.make_async_remote_copy(
            src_ref=source.at[rows], dst_ref=target.at[rows], send_sem=send.at[s - 1, h], recv_sem=recv.at[s - 1, h],
            device_id=to, device_id_type=MESH,
        )

    moves = {}

    def forward(s, h):
        for name, bufs, send, recv, to, far_half in (
            ("r", right, r_s, r_r, to_right, 0),
            ("l", left, l_s, l_r, to_left, 1),
        ):
            if s < half or (s == half and h == far_half):
                source = own if s == 1 else bufs[s - 1]
                moves[name, s, h] = hop(source, bufs[s], h, s, send, recv, to)
                moves[name, s, h].start()

    def serve(origin, buffer):
        for dk in range(1, GRP):
            k = (k_me + dk) % GRP
            picked[k, origin] = buffer[asked[k, 0, origin * GRP + k_me]]
            pltpu.make_async_remote_copy(
                src_ref=picked.at[k, origin], dst_ref=got_ref.at[k_me, origin],
                send_sem=x_s.at[dk - 1], recv_sem=x_r.at[dk - 1],
                device_id=(z * GRP + k, y), device_id_type=MESH,
            ).start()
        got_ref[k_me, origin] = buffer[asked[k_me, 0, origin * GRP + k_me]]

    for h in range(2):
        forward(1, h)
    serve(z, own)
    for s in range(1, half + 1):
        for h in range(2):
            for name in "rl":
                if (name, s, h) in moves:
                    moves[name, s, h].wait_recv()
            forward(s + 1, h)
        if s < half:
            serve((z + n_z - s) % n_z, right[s])
            serve((z + s) % n_z, left[s])
        else:
            serve((z + half) % n_z, far)
    for dk in range(1, GRP):
        k = (k_me + dk) % GRP
        pltpu.make_async_remote_copy(
            src_ref=picked.at[k], dst_ref=got_ref.at[k_me], send_sem=x_s.at[dk - 1], recv_sem=x_r.at[dk - 1],
            device_id=(z * GRP + k, y), device_id_type=MESH,
        ).wait()
    for copy in strips:
        copy.wait_send()
    for copy in moves.values():
        copy.wait_send()


def spread(n_z, part, prestress, friction, load_rate, asked):
    vm = pl.BlockSpec(memory_space=pltpu.VMEM)
    half = n_z // 2
    patches = (PATCH, BLOCK, PE)
    dma = pltpu.SemaphoreType.DMA
    return pl.pallas_call(
        functools.partial(spread_kernel, n_z),
        out_shape=(
            jax.ShapeDtypeStruct((GRP, n_z, BLOCK, PE), F32),
            jax.ShapeDtypeStruct(patches, F32),
        ),
        in_specs=[vm, vm, vm, vm, pl.BlockSpec(memory_space=pltpu.SMEM)],
        out_specs=(vm, vm),
        scratch_shapes=[
            pltpu.VMEM((SRC - 1,) + patches, F32),
            pltpu.VMEM(patches, F32),
            pltpu.VMEM((GRP, n_z, BLOCK, PE), F32),
            *[pltpu.VMEM(patches, F32) for _ in range(2 * (half - 1) + 1)],
            dma((SRC - 1,)), dma((SRC - 1,)),
            dma((half, 2)), dma((half, 2)), dma((half, 2)), dma((half, 2)),
            dma((GRP - 1,)), dma((GRP - 1,)),
        ],
        compiler_params=pltpu.CompilerParams(
            collective_id=1, has_side_effects=True, vmem_limit_bytes=VMEM_LIMIT
        ),
        name="spread",
    )(part, prestress, friction, load_rate, asked)


def finish_kernel(part_ref, pre_ref, fri_ref, load_ref, rate_ref, out_ref, parts, y_s, y_r):
    me, y = lax.axis_index("recv"), lax.axis_index("src")
    barrier = pltpu.get_barrier_semaphore()
    for dy in range(1, SRC):
        pl.semaphore_signal(barrier, inc=1, device_id=(me, (y + dy) % SRC), device_id_type=MESH)
    pl.semaphore_wait(barrier, SRC - 1)
    strips = start_strips(part_ref, parts, y_s, y_r)

    def early(p, carry):
        out_ref[p, 0:BLOCK] = solve_patch(p, 0, None, pre_ref, fri_ref, load_ref)
        out_ref[p, BLOCK : 2 * BLOCK] = rate_ref[p]
        return carry

    lax.fori_loop(0, PATCH, early, 0)
    for copy in strips:
        copy.wait()

    def late(p, carry):
        stress = part_ref[y * PATCH + p] + parts[0, p] + parts[1, p] + parts[2, p]
        out_ref[p, 2 * BLOCK :] = solve_patch(p, 2, stress, pre_ref, fri_ref, load_ref)
        return carry

    lax.fori_loop(0, PATCH, late, 0)


def finish(part, prestress, friction, load_rate, rates):
    vm = pl.BlockSpec(memory_space=pltpu.VMEM)
    dma = pltpu.SemaphoreType.DMA
    return pl.pallas_call(
        finish_kernel,
        out_shape=jax.ShapeDtypeStruct((PATCH, 3 * BLOCK, PE), F32),
        in_specs=[vm] * 5,
        out_specs=vm,
        scratch_shapes=[pltpu.VMEM((SRC - 1, PATCH, BLOCK, PE), F32), dma((SRC - 1,)), dma((SRC - 1,))],
        compiler_params=pltpu.CompilerParams(
            collective_id=2, has_side_effects=True, vmem_limit_bytes=VMEM_LIMIT
        ),
        name="finish",
    )(part, prestress, friction, load_rate, rates)


def local(interactions, list_lengths, kernels, prestress, friction, load_rate):
    n_z = lax.axis_size("recv") // GRP
    base = (lax.axis_index("recv") * (SRC * PATCH)).reshape(1)
    flat = kernels.reshape(KER, PE * LAGS, PE)
    table, weight, asked = ask(n_z, interactions, prestress, friction, load_rate, flat)
    part, early = first(n_z, interactions, list_lengths, base, table, weight)
    got, rates = spread(n_z, part, prestress, friction, load_rate, asked)
    part = second(n_z, interactions, list_lengths, base, got, weight, early)
    return finish(part, prestress, friction, load_rate, rates)


def solution(mesh):
    own = P(("recv", "src"))
    in_specs = (
        P(None, ("recv", "src")),
        own,
        P(("recv", "src"), None, None, None),
        P(("recv", "src"), None),
        P(("recv", "src"), None),
        P(("recv", "src"), None),
    )
    out_specs = P(("recv", "src"), None, None)
    return jax.shard_map(local, mesh=mesh, in_specs=in_specs, out_specs=out_specs, check_vma=False)
```

```python
import functools

import jax
import jax.numpy as jnp
from jax import lax
from jax.experimental import pallas as pl
from jax.experimental.pallas import tpu as pltpu
from jax.sharding import PartitionSpec as P

MESH = pl.DeviceIdType.MESH
F32 = jnp.float32
BF16 = jnp.bfloat16

PE = 128
LAGS = 16
BLOCK = 32
PATCH = 8
KER = 4
ENT = 24
NENT = KER * ENT
GRP = 8
SRC = 4
DAMP = 0.5
VMEM_LIMIT = 56 * 1024 * 1024
WIDE = 3 * LAGS * PE // 2
HALF = BLOCK // 2
PAD = 6


def recip(x):
    r = pl.reciprocal(x, approx=True)
    return r * (2.0 - x * r)


def newton(drive, friction, start=None):
    size = jnp.abs(drive) if start is None else drive
    v = size * (recip(DAMP + friction) if start is None else start)
    for _ in range(3):
        square = 1.0 + v * v
        root = lax.rsqrt(square)
        arc = jnp.log(v + square * root)
        v = (size + friction * (root * v - arc)) * recip(DAMP + friction * root)
    return jnp.where(drive < 0, -v, v) if start is None else v


def split(value):
    high = value.astype(BF16)
    return high, (value - high.astype(F32)).astype(BF16)


def ask_kernel(
    n_z, inter_ref, pre_ref, fri_ref, load_ref, kern_ref,
    table_ref, weight_ref, wanted_ref,
    zbuf, req, asked, picked, kern_f32, weight, req_s, req_r, z_s, z_r, x_s, x_r, loc, out_s,
):
    me, y = lax.axis_index("recv"), lax.axis_index("src")
    z, k_me = me // GRP, me % GRP
    barrier = pltpu.get_barrier_semaphore()
    for dz in range(1, n_z):
        pl.semaphore_signal(barrier, inc=1, device_id=(((z + dz) % n_z) * GRP + k_me, y), device_id_type=MESH)
    for dk in range(1, GRP):
        pl.semaphore_signal(barrier, inc=1, device_id=(z * GRP + (k_me + dk) % GRP, y), device_id_type=MESH)
    fetch = pltpu.make_async_copy(kern_ref, kern_f32, loc.at[0])
    fetch.start()
    zbuf[z, 0:8, :] = pre_ref[...]
    zbuf[z, 8:16, :] = fri_ref[...]
    zbuf[z, 16:24, :] = load_ref[...]
    row = inter_ref[1:2, :]
    eye = lax.broadcasted_iota(jnp.int32, (NENT, NENT), 0) == lax.broadcasted_iota(jnp.int32, (NENT, NENT), 1)
    column = jnp.sum(jnp.where(eye, jnp.broadcast_to(row, (NENT, NENT)), 0), axis=1, keepdims=True)
    owner = lax.shift_right_logical(column, 5)
    place = jnp.bitwise_and(column, PATCH - 1)
    hit = owner == lax.broadcasted_iota(jnp.int32, (NENT, n_z * GRP), 1)
    wanted = jnp.max(jnp.where(hit, place, 0), axis=0, keepdims=True)
    req[k_me] = jnp.broadcast_to(wanted, (8, n_z * GRP))
    pl.semaphore_wait(barrier, n_z - 1 + GRP - 1)
    sends = []
    for dk in range(1, GRP):
        sends.append(
            pltpu.make_async_remote_copy(
                src_ref=req.at[k_me], dst_ref=req.at[k_me], send_sem=req_s.at[dk - 1], recv_sem=req_r.at[dk - 1],
                device_id=(z * GRP + (k_me + dk) % GRP, y), device_id_type=MESH,
            )
        )
        sends[-1].start()
    zsends = []
    order = sorted(range(1, n_z), key=lambda d: -min(d, n_z - d))
    for dz in order:
        zsends.append(
            pltpu.make_async_remote_copy(
                src_ref=zbuf.at[z], dst_ref=zbuf.at[z], send_sem=z_s.at[dz - 1], recv_sem=z_r.at[dz - 1],
                device_id=(((z + dz) % n_z) * GRP + k_me, y), device_id_type=MESH,
            )
        )
        zsends[-1].start()
    fetch.wait()

    def weights(k, carry):
        for lag in range(LAGS):
            high, low = split(kern_f32[k, pl.ds(lag, PE, stride=LAGS), :].T)
            weight[k, lag * PE : (lag + 1) * PE, 0:PE] = high
            weight[k, lag * PE : (lag + 1) * PE, PE : 2 * PE] = low
            pair = lag // 2
            at, side = LAGS * PE + (pair // 2 * 2 + lag % 2) * PE, (pair % 2) * PE
            weight[k, at : at + PE, side : side + PE] = high
        return carry

    lax.fori_loop(0, KER, weights, 0)
    store = pltpu.make_async_copy(weight, weight_ref, out_s)
    store.start()
    for copy in sends:
        copy.wait()
    for k in range(GRP):
        wanted_ref[k : k + 1, :] = req[k, 0:1, :]
    down = pltpu.make_async_copy(wanted_ref, asked, loc.at[1])
    down.start()
    down.wait()
    for copy in zsends:
        copy.wait()

    def pick(k, carry):
        for zz in range(n_z):
            p = asked[k, zz * GRP + k_me]
            for i in range(3):
                picked[k, i, zz : zz + 1, :] = zbuf[zz, pl.ds(8 * i + p, 1), :]
        return carry

    lax.fori_loop(0, GRP, pick, 0)
    xsends = []
    for dk in range(1, GRP):
        k = (k_me + dk) % GRP
        xsends.append(
            pltpu.make_async_remote_copy(
                src_ref=picked.at[k], dst_ref=table_ref.at[k_me], send_sem=x_s.at[dk - 1], recv_sem=x_r.at[dk - 1],
                device_id=(z * GRP + k, y), device_id_type=MESH,
            )
        )
        xsends[-1].start()
    table_ref[k_me] = picked[k_me]
    for copy in xsends:
        copy.wait()
    store.wait()


def ask(n_z, interactions, prestress, friction, load_rate, kernels):
    vm = pl.BlockSpec(memory_space=pltpu.VMEM)
    owners = n_z * GRP
    return pl.pallas_call(
        functools.partial(ask_kernel, n_z),
        out_shape=(
            jax.ShapeDtypeStruct((GRP, 3, n_z, PE), F32),
            jax.ShapeDtypeStruct((KER, WIDE, 2 * PE), BF16),
            jax.ShapeDtypeStruct((GRP, owners), jnp.int32),
        ),
        in_specs=[vm, vm, vm, vm, pl.BlockSpec(memory_space=pl.ANY)],
        out_specs=(vm, pl.BlockSpec(memory_space=pl.ANY), vm),
        scratch_shapes=[
            pltpu.VMEM((n_z, 24, PE), F32),
            pltpu.VMEM((GRP, 8, owners), jnp.int32),
            pltpu.SMEM((GRP, owners), jnp.int32),
            pltpu.VMEM((GRP, 3, n_z, PE), F32),
            pltpu.VMEM((KER, LAGS * PE, PE), F32),
            pltpu.VMEM((KER, WIDE, 2 * PE), BF16),
            pltpu.SemaphoreType.DMA((GRP - 1,)),
            pltpu.SemaphoreType.DMA((GRP - 1,)),
            pltpu.SemaphoreType.DMA((n_z - 1,)),
            pltpu.SemaphoreType.DMA((n_z - 1,)),
            pltpu.SemaphoreType.DMA((GRP - 1,)),
            pltpu.SemaphoreType.DMA((GRP - 1,)),
            pltpu.SemaphoreType.DMA((2,)),
            pltpu.SemaphoreType.DMA,
        ],
        compiler_params=pltpu.CompilerParams(
            collective_id=0, has_side_effects=True, vmem_limit_bytes=VMEM_LIMIT
        ),
        name="ask",
    )(interactions, prestress, friction, load_rate, kernels)


def history_of(k, rows):
    pre, fri, load, delay = rows[k, 0], rows[k, 1], rows[k, 2], rows[k, 3]
    start = recip(DAMP + fri)

    def history(ahead):
        time = lax.convert_element_type(ahead, F32) - delay
        v = newton(pre + load * (time + 1.0), fri, start)
        return jnp.where((time >= 0.0) & (time < 32.0), v, 0.0)

    return history


def put(k, high_ref, low_ref, start, left, right):
    at = pl.ds(pl.multiple_of(start, 2 * ENT), 2 * ENT)
    high_ref[k, at, 0:PE], low_ref[k, at, 0:PE] = split(left)
    high_ref[k, at, PE : 2 * PE], low_ref[k, at, PE : 2 * PE] = split(right)


def conv(k, half, offset, skip, high_ref, low_ref, weight_ref, carry_ref, terms):
    def stacked(ref, t, times, pairs):
        starts = [(t + 14 - 2 * j - offset) * ENT for j in pairs]
        return jnp.concatenate([ref[k, start : start + times * ENT, :] for start in starts], axis=1)

    base = LAGS * PE
    if half:
        carry = carry_ref[k]
    elif skip:
        carry = jnp.zeros((2 * ENT, PE), F32)
    else:
        rest = jnp.dot(stacked(low_ref, -2, 2, (0, 2, 4, 6)), weight_ref[k, base:, :], preferred_element_type=F32)
        carry = rest[:, PE:]
    for t in range(half * HALF, half * HALF + HALF, 8):
        pairs = [j for j in range(8) if not skip or 2 * j <= t + 7]
        evens = pairs[::2]
        both = jnp.dot(stacked(high_ref, t, 8, pairs), weight_ref[k, 0 : len(pairs) * 2 * PE, :], preferred_element_type=F32)
        rest = jnp.dot(
            stacked(low_ref, t, 8, evens), weight_ref[k, base : base + len(evens) * 2 * PE, :], preferred_element_type=F32
        )
        late = jnp.concatenate([carry, rest[: 6 * ENT, PE:]], axis=0)
        carry = rest[6 * ENT :, PE:]
        terms[k, t * ENT : (t + 8) * ENT, :] = both[:, :PE] + both[:, PE:] + (rest[:, :PE] + late)
    if not half:
        carry_ref[k] = carry


def routes(inter_ref, length):
    me = lax.axis_index("recv")
    shape = (SRC * PATCH, NENT)
    hit = jnp.broadcast_to(inter_ref[0:1, :], shape) == lax.broadcasted_iota(jnp.int32, shape, 0) + me * (SRC * PATCH)
    live = lax.broadcasted_iota(jnp.int32, shape, 1) < length
    return jnp.where(hit & live, 1.0, 0.0).astype(BF16)


def route(half, route_ref, terms, part_ref):
    def pair(i, carry):
        t = half * HALF + 2 * i
        rows = [
            jnp.concatenate([terms[k, pl.ds(pl.multiple_of((t + j) * ENT, 8), ENT), :] for k in range(KER)], axis=0)
            for j in range(2)
        ]
        high, low = split(jnp.concatenate(rows, axis=1))
        both = jnp.dot(route_ref[...], high, preferred_element_type=F32)
        both = both + jnp.dot(route_ref[...], low, preferred_element_type=F32)
        part_ref[pl.ds(2 * i, SRC * PATCH, stride=HALF), :] = both[:, :PE]
        part_ref[pl.ds(2 * i + 1, SRC * PATCH, stride=HALF), :] = both[:, PE:]
        return carry

    lax.fori_loop(0, HALF // 2, pair, 0, unroll=2)


def start_weights(weight_hbm, weight, sems):
    copies = [pltpu.make_async_copy(weight_hbm.at[k], weight.at[k], sems.at[k]) for k in range(KER)]
    for copy in copies:
        copy.start()
    return copies


def start_strips(part_ref, parts, send, recv):
    me, y = lax.axis_index("recv"), lax.axis_index("src")
    rows = PATCH * HALF
    copies = []
    for dy in (2, 1, 3):
        to = (y + dy) % SRC
        copies.append(
            pltpu.make_async_remote_copy(
                src_ref=part_ref.at[pl.ds(to * rows, rows)], dst_ref=parts.at[dy - 1],
                send_sem=send.at[dy - 1], recv_sem=recv.at[dy - 1],
                device_id=(me, to), device_id_type=MESH,
            )
        )
        copies[-1].start()
    return copies


def strip_sum(p, part_ref, parts):
    y = lax.axis_index("src")
    own = part_ref[pl.ds(pl.multiple_of((y * PATCH + p) * HALF, HALF), HALF), :]
    at = pl.ds(pl.multiple_of(p * HALF, HALF), HALF)
    return own + parts[0, at, :] + parts[1, at, :] + parts[2, at, :]


def solve_patch(p, time, count, stress, pre_ref, fri_ref, load_ref):
    pre, fri, load = pre_ref[pl.ds(p, 1), :], fri_ref[pl.ds(p, 1), :], load_ref[pl.ds(p, 1), :]
    times = lax.broadcasted_iota(jnp.int32, (count, PE), 0).astype(F32) + float(time + 1)
    drive = pre + load * times
    if stress is not None:
        drive = drive + stress
    return newton(drive, jnp.broadcast_to(fri, (count, PE)))


PEERS = (4, 3, 5, 2, 6, 7, 1)
CUTS = 2


def spread_kernel(
    n_z, inter_ref, inter_rows, length_ref, table_ref, weight_hbm, pre_ref, fri_ref, load_ref, asked,
    got_ref, rate_ref, early_ref, *scratch
):
    half = n_z // 2
    rows, weight, w_s, high, low, carry_ref, terms, route_ref, picked = scratch[:9]
    part, parts, own = scratch[9:11], scratch[11:13], scratch[13:15]
    rest = scratch[15:]
    right = {s: rest[2 * s - 2 : 2 * s] for s in range(1, half)}
    left = {s: rest[2 * (half + s) - 4 : 2 * (half + s) - 2] for s in range(1, half)}
    far = rest[4 * half - 4 : 4 * half - 2]
    y_s, y_r, r_s, r_r, l_s, l_r, x_s, x_r, loc = rest[4 * half - 2 :]
    right[half] = left[half] = far
    right[0] = left[0] = own
    me, y = lax.axis_index("recv"), lax.axis_index("src")
    z, k_me = me // GRP, me % GRP
    to_right = (((z + 1) % n_z) * GRP + k_me, y)
    to_left = (((z + n_z - 1) % n_z) * GRP + k_me, y)
    barrier = pltpu.get_barrier_semaphore()
    for dy in range(1, SRC):
        pl.semaphore_signal(barrier, inc=1, device_id=(me, (y + dy) % SRC), device_id_type=MESH)
    for to in (to_right, to_left):
        pl.semaphore_signal(barrier, inc=1, device_id=to, device_id_type=MESH)
    for dk in range(1, GRP):
        pl.semaphore_signal(barrier, inc=1, device_id=(z * GRP + (k_me + dk) % GRP, y), device_id_type=MESH)

    copies = start_weights(weight_hbm, weight, w_s)
    route_ref[...] = routes(inter_rows, length_ref[0])
    for k in range(KER):
        high[k, 0 : PAD * ENT, :] = jnp.zeros((PAD * ENT, 2 * PE), BF16)
        low[k, 0 : PAD * ENT, :] = jnp.zeros((PAD * ENT, 2 * PE), BF16)

        def fill(e, carry):
            owner = lax.shift_right_logical(inter_ref[1, k * ENT + e], 5)
            zz, kk = owner // GRP, owner % GRP
            for i in range(3):
                rows[k, i, pl.ds(e, 1), :] = table_ref[kk, i, pl.ds(zz, 1), :]
            delay = inter_ref[2, k * ENT + e]
            rows[k, 3, pl.ds(e, 1), :] = jnp.full((1, PE), delay, jnp.int32).astype(F32)
            return carry

        lax.fori_loop(0, ENT, fill, 0, unroll=8)
        history = history_of(k, rows)

        def pair(i, before):
            now, after = history(32 + 2 * i), history(33 + 2 * i)
            side = jnp.concatenate([now, after], axis=0)
            put(k, high, low, (PAD + 2 * i) * ENT, side, jnp.concatenate([before, now], axis=0))
            return after

        lax.fori_loop(0, 16, pair, jnp.zeros((ENT, PE), F32))

    strips = []
    for th in range(2):
        for k in range(KER):
            if th == 0:
                copies[k].wait()
            conv(k, th, 14 - PAD, True, high, low, weight, carry_ref, terms)
        route(th, route_ref, terms, part[th])
        if th == 0:
            pl.semaphore_wait(barrier, SRC - 1 + 2 + GRP - 1)
        strips.append(start_strips(part[th], parts[th], y_s.at[th], y_r.at[th]))

    moves = {}

    def forward(s, th, h):
        for name, bufs, send, recv, to in (("r", right, r_s, r_r, to_right), ("l", left, l_s, l_r, to_left)):
            if s < half or (s == half and (h < CUTS // 2) == (name == "r")):
                at = pl.ds(h * (PATCH // CUTS), PATCH // CUTS)
                moves[name, s, th, h] = pltpu.make_async_remote_copy(
                    src_ref=bufs[s - 1][th].at[at], dst_ref=bufs[s][th].at[at],
                    send_sem=send.at[s - 1, th * CUTS + h], recv_sem=recv.at[s - 1, th * CUTS + h],
                    device_id=to, device_id_type=MESH,
                )
                moves[name, s, th, h].start()

    def pick(origin, slot, buffers):
        for k in range(GRP):
            for th in range(2):
                picked[k, slot, th * HALF : (th + 1) * HALF] = buffers[th][asked[k, origin * GRP + k_me]]

    def to_peers(first, count):
        for dk in PEERS:
            k = (k_me + dk) % GRP
            pltpu.make_async_remote_copy(
                src_ref=picked.at[k, pl.ds(first, count)], dst_ref=got_ref.at[k_me, pl.ds(first, count)],
                send_sem=x_s.at[dk - 1], recv_sem=x_r.at[dk - 1],
                device_id=(z * GRP + k, y), device_id_type=MESH,
            ).start()

    def early(i):
        def one(k, carry):
            history = history_of(k, rows)
            for b in range(4 * i, 4 * i + 4, 2):
                early_ref[k, b * ENT : (b + 2) * ENT, :] = jnp.concatenate([history(b + 48), history(b + 49)], axis=0)
            return carry

        lax.fori_loop(0, KER, one, 0)

    for th in range(2):
        for copy in strips[th]:
            copy.wait_recv()

        def solve(p, carry):
            v = solve_patch(p, BLOCK + th * HALF, HALF, strip_sum(p, part[th], parts[th]), pre_ref, fri_ref, load_ref)
            own[th][p] = v
            rate_ref[p, th * HALF : (th + 1) * HALF] = v
            return carry

        lax.fori_loop(0, PATCH, solve, 0)
        for h in range(CUTS):
            forward(1, th, h)
    pick(z, 0, own)
    to_peers(0, 1)
    for s in range(1, half + 1):
        early(s - 1)
        for th in range(2):
            for h in range(CUTS):
                for name in "rl":
                    if (name, s, th, h) in moves:
                        moves[name, s, th, h].wait_recv()
                forward(s + 1, th, h)
        if s < half:
            pick((z + n_z - s) % n_z, 2 * s - 1, right[s])
            pick((z + s) % n_z, 2 * s, left[s])
            to_peers(2 * s - 1, 2)
        else:
            pick((z + half) % n_z, n_z - 1, far)
            to_peers(n_z - 1, 1)
    mine = pltpu.make_async_copy(picked.at[k_me], got_ref.at[k_me], loc)
    mine.start()
    for dk in range(1, GRP):
        k = (k_me + dk) % GRP
        pltpu.make_async_remote_copy(
            src_ref=picked.at[k], dst_ref=got_ref.at[k_me], send_sem=x_s.at[dk - 1], recv_sem=x_r.at[dk - 1],
            device_id=(z * GRP + k, y), device_id_type=MESH,
        ).wait()
    mine.wait()
    for copy in (*strips[0], *strips[1], *moves.values()):
        copy.wait_send()


def spread(n_z, interactions, lengths, table, weight, prestress, friction, load_rate, asked):
    vm = pl.BlockSpec(memory_space=pltpu.VMEM)
    sm = pl.BlockSpec(memory_space=pltpu.SMEM)
    hbm = pl.BlockSpec(memory_space=pl.ANY)
    half = n_z // 2
    dma = pltpu.SemaphoreType.DMA
    halves = pltpu.VMEM((PATCH, HALF, PE), F32)
    return pl.pallas_call(
        functools.partial(spread_kernel, n_z),
        out_shape=(
            jax.ShapeDtypeStruct((GRP, n_z, BLOCK, PE), F32),
            jax.ShapeDtypeStruct((PATCH, BLOCK, PE), F32),
            jax.ShapeDtypeStruct((KER, BLOCK * ENT, PE), F32),
        ),
        in_specs=[sm, vm, sm, vm, hbm, vm, vm, vm, sm],
        out_specs=(hbm, vm, vm),
        scratch_shapes=[
            pltpu.VMEM((KER, 4, ENT, PE), F32),
            *compute_scratch(PAD + 32),
            pltpu.VMEM((GRP, n_z, BLOCK, PE), F32),
            *strip_scratch(),
            halves, halves,
            *[halves for _ in range(2 * (2 * (half - 1) + 1))],
            dma((2, SRC - 1)), dma((2, SRC - 1)),
            *[dma((half, 2 * CUTS)) for _ in range(4)],
            dma((GRP - 1,)), dma((GRP - 1,)), dma,
        ],
        compiler_params=pltpu.CompilerParams(
            collective_id=1, has_side_effects=True, vmem_limit_bytes=VMEM_LIMIT
        ),
        name="spread",
    )(interactions, interactions, lengths, table, weight, prestress, friction, load_rate, asked)


def compute_scratch(blocks):
    return [
        pltpu.VMEM((KER, WIDE, 2 * PE), BF16),
        pltpu.SemaphoreType.DMA((KER,)),
        pltpu.VMEM((KER, blocks * ENT, 2 * PE), BF16),
        pltpu.VMEM((KER, blocks * ENT, 2 * PE), BF16),
        pltpu.VMEM((KER, 2 * ENT, PE), F32),
        pltpu.VMEM((KER, BLOCK * ENT, PE), F32),
        pltpu.VMEM((SRC * PATCH, NENT), BF16),
    ]


def strip_scratch():
    part = pltpu.VMEM((SRC * PATCH * HALF, PE), F32)
    parts = pltpu.VMEM((SRC - 1, PATCH * HALF, PE), F32)
    return [part, part, parts, parts]


def finish_kernel(
    n_z, inter_ref, inter_rows, length_ref, got_hbm, weight_hbm, early_ref, pre_ref, fri_ref, load_ref, rate_ref, out_ref,
    got_ref, loc, line, weight, w_s, high, low, carry_ref, terms, route_ref, part_a, part_b, parts_a, parts_b, y_s, y_r,
):
    me, y = lax.axis_index("recv"), lax.axis_index("src")
    z = me // GRP
    part, parts = (part_a, part_b), (parts_a, parts_b)
    barrier = pltpu.get_barrier_semaphore()
    for dy in range(1, SRC):
        pl.semaphore_signal(barrier, inc=1, device_id=(me, (y + dy) % SRC), device_id_type=MESH)
    fetch = pltpu.make_async_copy(got_hbm, got_ref.at[:, :, pl.ds(HALF, BLOCK)], loc)
    fetch.start()
    copies = start_weights(weight_hbm, weight, w_s)
    route_ref[...] = routes(inter_rows, length_ref[0])

    def clear(k, carry):
        got_ref[k, :, 0:HALF, :] = jnp.zeros((n_z, HALF, PE), F32)
        return carry

    lax.fori_loop(0, GRP, clear, 0)

    def known(p, carry):
        out_ref[p, 0:BLOCK] = solve_patch(p, 0, BLOCK, None, pre_ref, fri_ref, load_ref)
        out_ref[p, BLOCK : 2 * BLOCK] = rate_ref[p]
        return carry

    lax.fori_loop(0, PATCH, known, 0)
    fetch.wait()
    for k in range(KER):
        line[0 : 32 * ENT, :] = early_ref[k]
        line[32 * ENT : 48 * ENT, :] = jnp.zeros((16 * ENT, PE), F32)

        def place(e, carry):
            owner = lax.shift_right_logical(inter_ref[1, k * ENT + e], 5)
            delay = inter_ref[2, k * ENT + e]
            ahead = (owner // GRP - z + n_z) % n_z
            slot = jnp.where(ahead < n_z // 2, 2 * ahead, 2 * (n_z - ahead) - 1)
            line[pl.ds(16 * ENT + e, BLOCK, stride=ENT), :] += got_ref[owner % GRP, slot, pl.ds(jnp.clip(48 - delay, 0, HALF), BLOCK), :]
            return carry

        lax.fori_loop(0, ENT, place, 0, unroll=8)

        def pair(i, carry):
            left = line[pl.ds(pl.multiple_of((2 * i + 2) * ENT, 2 * ENT), 2 * ENT), :]
            right = line[pl.ds(pl.multiple_of((2 * i + 1) * ENT, ENT), 2 * ENT), :]
            put(k, high, low, 2 * i * ENT, left, right)
            return carry

        lax.fori_loop(0, 23, pair, 0)

    strips = []
    for th in range(2):
        for k in range(KER):
            if th == 0:
                copies[k].wait()
            conv(k, th, 0, False, high, low, weight, carry_ref, terms)
        route(th, route_ref, terms, part[th])
        if th == 0:
            pl.semaphore_wait(barrier, SRC - 1)
        strips.append(start_strips(part[th], parts[th], y_s.at[th], y_r.at[th]))
    for th in range(2):
        for copy in strips[th]:
            copy.wait()

        def solve(p, carry):
            at = pl.ds(2 * BLOCK + th * HALF, HALF)
            stress = strip_sum(p, part[th], parts[th])
            out_ref[p, at] = solve_patch(p, 2 * BLOCK + th * HALF, HALF, stress, pre_ref, fri_ref, load_ref)
            return carry

        lax.fori_loop(0, PATCH, solve, 0)


def finish(n_z, interactions, lengths, got, weight, early, prestress, friction, load_rate, rates):
    vm = pl.BlockSpec(memory_space=pltpu.VMEM)
    sm = pl.BlockSpec(memory_space=pltpu.SMEM)
    hbm = pl.BlockSpec(memory_space=pl.ANY)
    dma = pltpu.SemaphoreType.DMA
    return pl.pallas_call(
        functools.partial(finish_kernel, n_z),
        out_shape=jax.ShapeDtypeStruct((PATCH, 3 * BLOCK, PE), F32),
        in_specs=[sm, vm, sm, hbm, hbm, vm, vm, vm, vm, vm],
        out_specs=vm,
        scratch_shapes=[
            pltpu.VMEM((GRP, n_z, HALF + BLOCK, PE), F32),
            dma,
            pltpu.VMEM((48 * ENT, PE), F32),
            *compute_scratch(46),
            *strip_scratch(),
            dma((2, SRC - 1)), dma((2, SRC - 1)),
        ],
        compiler_params=pltpu.CompilerParams(
            collective_id=2, has_side_effects=True, vmem_limit_bytes=VMEM_LIMIT
        ),
        name="finish",
    )(interactions, interactions, lengths, got, weight, early, prestress, friction, load_rate, rates)


def local(interactions, list_lengths, kernels, prestress, friction, load_rate):
    n_z = lax.axis_size("recv") // GRP
    flat = kernels.reshape(KER, PE * LAGS, PE)
    own = (prestress, friction, load_rate)
    table, weight, asked = ask(n_z, interactions, *own, flat)
    got, rates, early = spread(n_z, interactions, list_lengths, table, weight, *own, asked)
    return finish(n_z, interactions, list_lengths, got, weight, early, *own, rates)


def solution(mesh):
    own = P(("recv", "src"))
    in_specs = (
        P(None, ("recv", "src")),
        own,
        P(("recv", "src"), None, None, None),
        P(("recv", "src"), None),
        P(("recv", "src"), None),
        P(("recv", "src"), None),
    )
    out_specs = P(("recv", "src"), None, None)
    return jax.shard_map(local, mesh=mesh, in_specs=in_specs, out_specs=out_specs, check_vma=False)
```

```python
import functools

import jax
import jax.numpy as jnp
from jax import lax
from jax.experimental import pallas as pl
from jax.experimental.pallas import tpu as pltpu
from jax.sharding import PartitionSpec as P

MESH = pl.DeviceIdType.MESH
F32 = jnp.float32
BF16 = jnp.bfloat16

PE = 128
LAGS = 16
BLOCK = 32
PATCH = 8
KER = 4
ENT = 24
NENT = KER * ENT
GRP = 8
SRC = 4
DAMP = 0.5
VMEM_LIMIT = 56 * 1024 * 1024
WIDE = 3 * LAGS * PE // 2
HALF = BLOCK // 2
PAD = 6


def recip(x):
    r = pl.reciprocal(x, approx=True)
    return r * (2.0 - x * r)


def newton(drive, friction, start=None):
    size = jnp.abs(drive) if start is None else drive
    v = size * (recip(DAMP + friction) if start is None else start)
    for _ in range(3):
        square = 1.0 + v * v
        root = lax.rsqrt(square)
        arc = jnp.log(v + square * root)
        v = (size + friction * (root * v - arc)) * recip(DAMP + friction * root)
    return jnp.where(drive < 0, -v, v) if start is None else v


def split(value):
    high = value.astype(BF16)
    return high, (value - high.astype(F32)).astype(BF16)


def history_of(k, rows):
    pre, fri, load, delay = rows[k, 0], rows[k, 1], rows[k, 2], rows[k, 3]
    start = recip(DAMP + fri)

    def history(ahead):
        time = lax.convert_element_type(ahead, F32) - delay
        v = newton(pre + load * (time + 1.0), fri, start)
        return jnp.where((time >= 0.0) & (time < 32.0), v, 0.0)

    return history


def put(k, high_ref, low_ref, start, left, right):
    at = pl.ds(pl.multiple_of(start, 2 * ENT), 2 * ENT)
    high_ref[k, at, 0:PE], low_ref[k, at, 0:PE] = split(left)
    high_ref[k, at, PE : 2 * PE], low_ref[k, at, PE : 2 * PE] = split(right)


def conv(k, half, offset, skip, high_ref, low_ref, weight_ref, carry_ref, terms):
    def stacked(ref, t, times, pairs):
        starts = [(t + 14 - 2 * j - offset) * ENT for j in pairs]
        return jnp.concatenate([ref[k, start : start + times * ENT, :] for start in starts], axis=1)

    base = LAGS * PE
    if half:
        carry = carry_ref[k]
    elif skip:
        carry = jnp.zeros((2 * ENT, PE), F32)
    else:
        rest = jnp.dot(stacked(low_ref, -2, 2, (0, 2, 4, 6)), weight_ref[k, base:, :], preferred_element_type=F32)
        carry = rest[:, PE:]
    for t in range(half * HALF, half * HALF + HALF, 8):
        pairs = [j for j in range(8) if not skip or 2 * j <= t + 7]
        evens = pairs[::2]
        both = jnp.dot(stacked(high_ref, t, 8, pairs), weight_ref[k, 0 : len(pairs) * 2 * PE, :], preferred_element_type=F32)
        rest = jnp.dot(
            stacked(low_ref, t, 8, evens), weight_ref[k, base : base + len(evens) * 2 * PE, :], preferred_element_type=F32
        )
        late = jnp.concatenate([carry, rest[: 6 * ENT, PE:]], axis=0)
        carry = rest[6 * ENT :, PE:]
        terms[k, t * ENT : (t + 8) * ENT, :] = both[:, :PE] + both[:, PE:] + (rest[:, :PE] + late)
    if not half:
        carry_ref[k] = carry


def routes(inter_ref, length):
    me = lax.axis_index("recv")
    shape = (SRC * PATCH, NENT)
    hit = jnp.broadcast_to(inter_ref[0:1, :], shape) == lax.broadcasted_iota(jnp.int32, shape, 0) + me * (SRC * PATCH)
    live = lax.broadcasted_iota(jnp.int32, shape, 1) < length
    return jnp.where(hit & live, 1.0, 0.0).astype(BF16)


def route(half, route_ref, terms, part_ref):
    def pair(i, carry):
        t = half * HALF + 2 * i
        rows = [
            jnp.concatenate([terms[k, pl.ds(pl.multiple_of((t + j) * ENT, 8), ENT), :] for k in range(KER)], axis=0)
            for j in range(2)
        ]
        high, low = split(jnp.concatenate(rows, axis=1))
        both = jnp.dot(route_ref[...], high, preferred_element_type=F32)
        both = both + jnp.dot(route_ref[...], low, preferred_element_type=F32)
        part_ref[pl.ds(2 * i, SRC * PATCH, stride=HALF), :] = both[:, :PE]
        part_ref[pl.ds(2 * i + 1, SRC * PATCH, stride=HALF), :] = both[:, PE:]
        return carry

    lax.fori_loop(0, HALF // 2, pair, 0, unroll=2)


def start_strips(part_ref, parts, send, recv):
    me, y = lax.axis_index("recv"), lax.axis_index("src")
    rows = PATCH * HALF
    copies = []
    for dy in (2, 1, 3):
        to = (y + dy) % SRC
        copies.append(
            pltpu.make_async_remote_copy(
                src_ref=part_ref.at[pl.ds(to * rows, rows)], dst_ref=parts.at[dy - 1],
                send_sem=send.at[dy - 1], recv_sem=recv.at[dy - 1],
                device_id=(me, to), device_id_type=MESH,
            )
        )
        copies[-1].start()
    return copies


def strip_sum(p, part_ref, parts):
    y = lax.axis_index("src")
    own = part_ref[pl.ds(pl.multiple_of((y * PATCH + p) * HALF, HALF), HALF), :]
    at = pl.ds(pl.multiple_of(p * HALF, HALF), HALF)
    return own + parts[0, at, :] + parts[1, at, :] + parts[2, at, :]


def solve_patch(p, time, count, stress, pre_ref, fri_ref, load_ref):
    pre, fri, load = pre_ref[pl.ds(p, 1), :], fri_ref[pl.ds(p, 1), :], load_ref[pl.ds(p, 1), :]
    times = lax.broadcasted_iota(jnp.int32, (count, PE), 0).astype(F32) + float(time + 1)
    drive = pre + load * times
    if stress is not None:
        drive = drive + stress
    return newton(drive, jnp.broadcast_to(fri, (count, PE)))


PEERS = (4, 3, 5, 2, 6, 7, 1)
CUTS = 2
STEP = 4


def rupture_kernel(
    n_z, inter_ref, inter_rows, length_ref, pre_ref, fri_ref, load_ref, kern_ref, out_ref,
    zbuf, req, wanted_ref, asked, chosen, table_ref, kern_f32, early_ref, got_ref, line,
    rows, weight, high, low, carry_ref, terms, route_ref, picked, *rest
):
    half, quarter = n_z // 2, n_z // STEP
    part, parts, own, rest = rest[0:4], rest[4:8], rest[8:10], rest[10:]
    right = {s: rest[2 * s - 2 : 2 * s] for s in range(1, half)}
    left = {s: rest[2 * (half + s) - 4 : 2 * (half + s) - 2] for s in range(1, half)}
    far = rest[4 * half - 4 : 4 * half - 2]
    req_s, req_r, z_s, z_r, ask_s, ask_r, y_s, y_r, r_s, r_r, l_s, l_r, x_s, x_r, loc = rest[4 * half - 2 :]
    right[half] = left[half] = far
    right[0] = left[0] = own
    me, y = lax.axis_index("recv"), lax.axis_index("src")
    z, k_me = me // GRP, me % GRP

    def at_z(dz):
        return (((z + dz + n_z) % n_z) * GRP + k_me, y)

    to_right, to_left = at_z(1), at_z(-1)
    barrier = pltpu.get_barrier_semaphore()
    for dy in range(1, SRC):
        pl.semaphore_signal(barrier, inc=1, device_id=(me, (y + dy) % SRC), device_id_type=MESH)
    for dz in (*range(STEP, n_z, STEP), 1, -1, -2):
        pl.semaphore_signal(barrier, inc=1, device_id=at_z(dz), device_id_type=MESH)
    for dk in range(1, GRP):
        pl.semaphore_signal(barrier, inc=1, device_id=(z * GRP + (k_me + dk) % GRP, y), device_id_type=MESH)
    fetch = pltpu.make_async_copy(kern_ref, kern_f32, loc.at[0])
    fetch.start()

    mine_at = (z % STEP) * quarter + z // STEP
    zbuf[mine_at, 0:8, :] = pre_ref[...]
    zbuf[mine_at, 8:16, :] = fri_ref[...]
    zbuf[mine_at, 16:24, :] = load_ref[...]
    row = inter_rows[1:2, :]
    eye = lax.broadcasted_iota(jnp.int32, (NENT, NENT), 0) == lax.broadcasted_iota(jnp.int32, (NENT, NENT), 1)
    column = jnp.sum(jnp.where(eye, jnp.broadcast_to(row, (NENT, NENT)), 0), axis=1, keepdims=True)
    owner_of = lax.shift_right_logical(column, 5)
    place_of = jnp.bitwise_and(column, PATCH - 1)
    hit = owner_of == lax.broadcasted_iota(jnp.int32, (NENT, n_z * GRP), 1)
    wanted = jnp.max(jnp.where(hit, place_of, 0), axis=0, keepdims=True)
    req[k_me] = jnp.broadcast_to(wanted, (8, n_z * GRP))
    route_ref[...] = routes(inter_rows, length_ref[0])

    def clear(k, carry):
        got_ref[k, :, 0:HALF, :] = jnp.zeros((n_z, HALF, PE), F32)
        return carry

    lax.fori_loop(0, GRP, clear, 0)
    pl.semaphore_wait(barrier, SRC - 1 + quarter - 1 + 3 + GRP - 1)

    def params(at, i, to):
        copy = pltpu.make_async_remote_copy(
            src_ref=zbuf.at[at], dst_ref=zbuf.at[at], send_sem=z_s.at[i], recv_sem=z_r.at[i],
            device_id=to, device_id_type=MESH,
        )
        copy.start()
        return copy

    near = [params(pl.ds(mine_at, 1), i - 1, at_z(i * STEP)) for i in sorted(range(1, quarter), key=lambda i: -min(i, quarter - i))]
    sends = []
    for dk in range(1, GRP):
        sends.append(
            pltpu.make_async_remote_copy(
                src_ref=req.at[k_me], dst_ref=req.at[k_me], send_sem=req_s.at[dk - 1], recv_sem=req_r.at[dk - 1],
                device_id=(z * GRP + (k_me + dk) % GRP, y), device_id_type=MESH,
            )
        )
        sends[-1].start()

    def weights(k, carry):
        for lag in range(LAGS):
            up, down = split(kern_f32[k, pl.ds(lag, PE, stride=LAGS), :].T)
            weight[k, lag * PE : (lag + 1) * PE, 0:PE] = up
            weight[k, lag * PE : (lag + 1) * PE, PE : 2 * PE] = down
            pair = lag // 2
            at, side = LAGS * PE + (pair // 2 * 2 + lag % 2) * PE, (pair % 2) * PE
            weight[k, at : at + PE, side : side + PE] = up
        return carry

    for copy in near:
        copy.wait_recv()
    group = pl.ds((z % STEP) * quarter, quarter)
    others = [params(group, quarter - 1 + i, at_z(dz)) for i, dz in enumerate((2, 1, -1))]
    fetch.wait()
    lax.fori_loop(0, KER, weights, 0)
    for copy in sends:
        copy.wait()
    for k in range(GRP):
        wanted_ref[k : k + 1, :] = req[k, 0:1, :]
    fall = pltpu.make_async_copy(wanted_ref, asked, loc.at[1])
    fall.start()
    fall.wait()
    for copy in others:
        copy.wait()
    for copy in near:
        copy.wait_send()

    def choose(k, carry):
        for zz in range(n_z):
            p = asked[k, zz * GRP + k_me]
            for i in range(3):
                chosen[k, i, zz : zz + 1, :] = zbuf[(zz % STEP) * quarter + zz // STEP, pl.ds(8 * i + p, 1), :]
        return carry

    lax.fori_loop(0, GRP, choose, 0)
    xsends = []
    for dk in PEERS:
        k = (k_me + dk) % GRP
        xsends.append(
            pltpu.make_async_remote_copy(
                src_ref=chosen.at[k], dst_ref=table_ref.at[k_me], send_sem=ask_s.at[dk - 1], recv_sem=ask_r.at[dk - 1],
                device_id=(z * GRP + k, y), device_id_type=MESH,
            )
        )
        xsends[-1].start()
    table_ref[k_me] = chosen[k_me]

    def known(p, carry):
        out_ref[p, 0:BLOCK] = solve_patch(p, 0, BLOCK, None, pre_ref, fri_ref, load_ref)
        return carry

    lax.fori_loop(0, PATCH, known, 0)
    for copy in xsends:
        copy.wait()

    for k in range(KER):
        high[k, 0 : PAD * ENT, :] = jnp.zeros((PAD * ENT, 2 * PE), BF16)
        low[k, 0 : PAD * ENT, :] = jnp.zeros((PAD * ENT, 2 * PE), BF16)

        def fill(e, carry):
            owner = lax.shift_right_logical(inter_ref[1, k * ENT + e], 5)
            zz, kk = owner // GRP, owner % GRP
            for i in range(3):
                rows[k, i, pl.ds(e, 1), :] = table_ref[kk, i, pl.ds(zz, 1), :]
            delay = inter_ref[2, k * ENT + e]
            rows[k, 3, pl.ds(e, 1), :] = jnp.full((1, PE), delay, jnp.int32).astype(F32)
            return carry

        lax.fori_loop(0, ENT, fill, 0, unroll=8)
        history = history_of(k, rows)

        def pair(i, before):
            now, after = history(32 + 2 * i), history(33 + 2 * i)
            side = jnp.concatenate([now, after], axis=0)
            put(k, high, low, (PAD + 2 * i) * ENT, side, jnp.concatenate([before, now], axis=0))
            return after

        lax.fori_loop(0, 16, pair, jnp.zeros((ENT, PE), F32))

    strips = []
    for th in range(2):
        for k in range(KER):
            conv(k, th, 14 - PAD, True, high, low, weight, carry_ref, terms)
        route(th, route_ref, terms, part[th])
        strips.append(start_strips(part[th], parts[th], y_s.at[th], y_r.at[th]))

    moves = {}

    def forward(s, th, h):
        for name, bufs, send, recv, to in (("r", right, r_s, r_r, to_right), ("l", left, l_s, l_r, to_left)):
            if s < half or (s == half and (h < CUTS // 2) == (name == "r")):
                at = pl.ds(h * (PATCH // CUTS), PATCH // CUTS)
                moves[name, s, th, h] = pltpu.make_async_remote_copy(
                    src_ref=bufs[s - 1][th].at[at], dst_ref=bufs[s][th].at[at],
                    send_sem=send.at[s - 1, th * CUTS + h], recv_sem=recv.at[s - 1, th * CUTS + h],
                    device_id=to, device_id_type=MESH,
                )
                moves[name, s, th, h].start()

    def pick(origin, slot, buffers):
        for k in range(GRP):
            for th in range(2):
                picked[k, slot, th * HALF : (th + 1) * HALF] = buffers[th][asked[k, origin * GRP + k_me]]

    def to_peers(first, count):
        for dk in PEERS:
            k = (k_me + dk) % GRP
            pltpu.make_async_remote_copy(
                src_ref=picked.at[k, pl.ds(first, count)], dst_ref=got_ref.at[k_me, pl.ds(first, count), pl.ds(HALF, BLOCK)],
                send_sem=x_s.at[dk - 1], recv_sem=x_r.at[dk - 1],
                device_id=(z * GRP + k, y), device_id_type=MESH,
            ).start()

    def early(i):
        def one(k, carry):
            history = history_of(k, rows)
            for b in range(4 * i, 4 * i + 4, 2):
                early_ref[k, b * ENT : (b + 2) * ENT, :] = jnp.concatenate([history(b + 48), history(b + 49)], axis=0)
            return carry

        lax.fori_loop(0, KER, one, 0)

    for th in range(2):
        for copy in strips[th]:
            copy.wait_recv()

        def solve(p, carry):
            v = solve_patch(p, BLOCK + th * HALF, HALF, strip_sum(p, part[th], parts[th]), pre_ref, fri_ref, load_ref)
            own[th][p] = v
            out_ref[p, BLOCK + th * HALF : BLOCK + (th + 1) * HALF] = v
            return carry

        lax.fori_loop(0, PATCH, solve, 0)
        for h in range(CUTS):
            forward(1, th, h)
    pick(z, 0, own)
    to_peers(0, 1)
    for s in range(1, half + 1):
        early(s - 1)
        for th in range(2):
            for h in range(CUTS):
                for name in "rl":
                    if (name, s, th, h) in moves:
                        moves[name, s, th, h].wait_recv()
                forward(s + 1, th, h)
        if s < half:
            pick((z + n_z - s) % n_z, 2 * s - 1, right[s])
            pick((z + s) % n_z, 2 * s, left[s])
            to_peers(2 * s - 1, 2)
        else:
            pick((z + half) % n_z, n_z - 1, far)
            to_peers(n_z - 1, 1)
    mine = pltpu.make_async_copy(picked.at[k_me], got_ref.at[k_me, :, pl.ds(HALF, BLOCK)], loc.at[2])
    mine.start()
    for dk in range(1, GRP):
        k = (k_me + dk) % GRP
        pltpu.make_async_remote_copy(
            src_ref=picked.at[k], dst_ref=got_ref.at[k_me, :, pl.ds(HALF, BLOCK)], send_sem=x_s.at[dk - 1], recv_sem=x_r.at[dk - 1],
            device_id=(z * GRP + k, y), device_id_type=MESH,
        ).wait()
    mine.wait()

    for k in range(KER):
        line[0 : 32 * ENT, :] = early_ref[k]
        line[32 * ENT : 48 * ENT, :] = jnp.zeros((16 * ENT, PE), F32)

        def place(e, carry):
            owner = lax.shift_right_logical(inter_ref[1, k * ENT + e], 5)
            delay = inter_ref[2, k * ENT + e]
            ahead = (owner // GRP - z + n_z) % n_z
            slot = jnp.where(ahead < n_z // 2, 2 * ahead, 2 * (n_z - ahead) - 1)
            line[pl.ds(16 * ENT + e, BLOCK, stride=ENT), :] += got_ref[owner % GRP, slot, pl.ds(jnp.clip(48 - delay, 0, HALF), BLOCK), :]
            return carry

        lax.fori_loop(0, ENT, place, 0, unroll=8)

        def pair(i, carry):
            left = line[pl.ds(pl.multiple_of((2 * i + 2) * ENT, 2 * ENT), 2 * ENT), :]
            right = line[pl.ds(pl.multiple_of((2 * i + 1) * ENT, ENT), 2 * ENT), :]
            put(k, high, low, 2 * i * ENT, left, right)
            return carry

        lax.fori_loop(0, 23, pair, 0)

    for th in range(2):
        for k in range(KER):
            conv(k, th, 0, False, high, low, weight, carry_ref, terms)
        route(th, route_ref, terms, part[2 + th])
        strips.append(start_strips(part[2 + th], parts[2 + th], y_s.at[2 + th], y_r.at[2 + th]))
    for th in range(2):
        for copy in strips[2 + th]:
            copy.wait_recv()

        def solve(p, carry):
            at = pl.ds(2 * BLOCK + th * HALF, HALF)
            stress = strip_sum(p, part[2 + th], parts[2 + th])
            out_ref[p, at] = solve_patch(p, 2 * BLOCK + th * HALF, HALF, stress, pre_ref, fri_ref, load_ref)
            return carry

        lax.fori_loop(0, PATCH, solve, 0)
    for copy in moves.values():
        copy.wait_send()
    for group in strips:
        for copy in group:
            copy.wait_send()


def local(interactions, list_lengths, kernels, prestress, friction, load_rate):
    n_z = lax.axis_size("recv") // GRP
    half = n_z // 2
    owners = n_z * GRP
    vm = pl.BlockSpec(memory_space=pltpu.VMEM)
    sm = pl.BlockSpec(memory_space=pltpu.SMEM)
    dma = pltpu.SemaphoreType.DMA
    part = pltpu.VMEM((SRC * PATCH * HALF, PE), F32)
    parts = pltpu.VMEM((SRC - 1, PATCH * HALF, PE), F32)
    halves = pltpu.VMEM((PATCH, HALF, PE), F32)
    peers = dma((GRP - 1,))
    return pl.pallas_call(
        functools.partial(rupture_kernel, n_z),
        out_shape=jax.ShapeDtypeStruct((PATCH, 3 * BLOCK, PE), F32),
        in_specs=[sm, vm, sm, vm, vm, vm, pl.BlockSpec(memory_space=pl.ANY)],
        out_specs=vm,
        scratch_shapes=[
            pltpu.VMEM((n_z, 24, PE), F32),
            pltpu.VMEM((GRP, 8, owners), jnp.int32),
            pltpu.VMEM((GRP, owners), jnp.int32),
            pltpu.SMEM((GRP, owners), jnp.int32),
            pltpu.VMEM((GRP, 3, n_z, PE), F32),
            pltpu.VMEM((GRP, 3, n_z, PE), F32),
            pltpu.VMEM((KER, LAGS * PE, PE), F32),
            pltpu.VMEM((KER, BLOCK * ENT, PE), F32),
            pltpu.VMEM((GRP, n_z, HALF + BLOCK, PE), F32),
            pltpu.VMEM((48 * ENT, PE), F32),
            pltpu.VMEM((KER, 4, ENT, PE), F32),
            pltpu.VMEM((KER, WIDE, 2 * PE), BF16),
            pltpu.VMEM((KER, 46 * ENT, 2 * PE), BF16),
            pltpu.VMEM((KER, 46 * ENT, 2 * PE), BF16),
            pltpu.VMEM((KER, 2 * ENT, PE), F32),
            pltpu.VMEM((KER, BLOCK * ENT, PE), F32),
            pltpu.VMEM((SRC * PATCH, NENT), BF16),
            pltpu.VMEM((GRP, n_z, BLOCK, PE), F32),
            part, part, part, part, parts, parts, parts, parts,
            *[halves for _ in range(2 + 2 * (2 * (half - 1) + 1))],
            peers, peers, dma((n_z // STEP + 2,)), dma((n_z // STEP + 2,)), peers, peers,
            dma((4, SRC - 1)), dma((4, SRC - 1)),
            *[dma((half, 2 * CUTS)) for _ in range(4)],
            peers, peers, dma((3,)),
        ],
        compiler_params=pltpu.CompilerParams(
            collective_id=0, has_side_effects=True, vmem_limit_bytes=VMEM_LIMIT
        ),
        name="rupture",
    )(interactions, interactions, list_lengths, prestress, friction, load_rate, kernels.reshape(KER, PE * LAGS, PE))


def solution(mesh):
    own = P(("recv", "src"))
    in_specs = (
        P(None, ("recv", "src")),
        own,
        P(("recv", "src"), None, None, None),
        P(("recv", "src"), None),
        P(("recv", "src"), None),
        P(("recv", "src"), None),
    )
    out_specs = P(("recv", "src"), None, None)
    return jax.shard_map(local, mesh=mesh, in_specs=in_specs, out_specs=out_specs, check_vma=False)
```

```python
import functools

import jax
import jax.numpy as jnp
from jax import lax
from jax.experimental import pallas as pl
from jax.experimental.pallas import tpu as pltpu
from jax.sharding import PartitionSpec as P

MESH = pl.DeviceIdType.MESH
F32 = jnp.float32
BF16 = jnp.bfloat16

PE = 128
LAGS = 16
BLOCK = 32
PATCH = 8
KER = 4
ENT = 24
NENT = KER * ENT
GRP = 8
SRC = 4
DAMP = 0.5
VMEM_LIMIT = 56 * 1024 * 1024
WIDE = 3 * LAGS * PE // 2
HALF = BLOCK // 2
PAD = 6


def recip(x):
    r = pl.reciprocal(x, approx=True)
    return r * (2.0 - x * r)


def newton(drive, friction, start=None):
    size = jnp.abs(drive) if start is None else drive
    v = size * (recip(DAMP + friction) if start is None else start)
    for _ in range(3):
        square = 1.0 + v * v
        root = lax.rsqrt(square)
        arc = jnp.log(v + square * root)
        v = (size + friction * (root * v - arc)) * recip(DAMP + friction * root)
    return jnp.where(drive < 0, -v, v) if start is None else v


def split(value):
    high = value.astype(BF16)
    return high, (value - high.astype(F32)).astype(BF16)


def history_of(k, rows):
    pre, fri, load, delay = rows[k, 0], rows[k, 1], rows[k, 2], rows[k, 3]
    start = recip(DAMP + fri)

    def history(ahead):
        time = lax.convert_element_type(ahead, F32) - delay
        v = newton(pre + load * (time + 1.0), fri, start)
        return jnp.where((time >= 0.0) & (time < 32.0), v, 0.0)

    return history


def put(k, high_ref, low_ref, start, left, right):
    at = pl.ds(pl.multiple_of(start, 2 * ENT), 2 * ENT)
    high_ref[k, at, 0:PE], low_ref[k, at, 0:PE] = split(left)
    high_ref[k, at, PE : 2 * PE], low_ref[k, at, PE : 2 * PE] = split(right)


def conv(k, half, offset, skip, high_ref, low_ref, weight_ref, carry_ref, terms):
    def stacked(ref, t, times, pairs):
        starts = [(t + 14 - 2 * j - offset) * ENT for j in pairs]
        return jnp.concatenate([ref[k, start : start + times * ENT, :] for start in starts], axis=1)

    base = LAGS * PE
    if half:
        carry = carry_ref[k]
    elif skip:
        carry = jnp.zeros((2 * ENT, PE), F32)
    else:
        rest = jnp.dot(stacked(low_ref, -2, 2, (0, 2, 4, 6)), weight_ref[k, base:, :], preferred_element_type=F32)
        carry = rest[:, PE:]
    for t in range(half * HALF, half * HALF + HALF, 8):
        pairs = [j for j in range(8) if not skip or 2 * j <= t + 7]
        evens = pairs[::2]
        both = jnp.dot(stacked(high_ref, t, 8, pairs), weight_ref[k, 0 : len(pairs) * 2 * PE, :], preferred_element_type=F32)
        rest = jnp.dot(
            stacked(low_ref, t, 8, evens), weight_ref[k, base : base + len(evens) * 2 * PE, :], preferred_element_type=F32
        )
        late = jnp.concatenate([carry, rest[: 6 * ENT, PE:]], axis=0)
        carry = rest[6 * ENT :, PE:]
        terms[k, t * ENT : (t + 8) * ENT, :] = both[:, :PE] + both[:, PE:] + (rest[:, :PE] + late)
    if not half:
        carry_ref[k] = carry


def routes(inter_ref, length):
    me = lax.axis_index("recv")
    shape = (SRC * PATCH, NENT)
    hit = jnp.broadcast_to(inter_ref[0:1, :], shape) == lax.broadcasted_iota(jnp.int32, shape, 0) + me * (SRC * PATCH)
    live = lax.broadcasted_iota(jnp.int32, shape, 1) < length
    return jnp.where(hit & live, 1.0, 0.0).astype(BF16)


def route(half, route_ref, terms, part_ref):
    def pair(i, carry):
        t = half * HALF + 2 * i
        rows = [
            jnp.concatenate([terms[k, pl.ds(pl.multiple_of((t + j) * ENT, 8), ENT), :] for k in range(KER)], axis=0)
            for j in range(2)
        ]
        high, low = split(jnp.concatenate(rows, axis=1))
        both = jnp.dot(route_ref[...], high, preferred_element_type=F32)
        both = both + jnp.dot(route_ref[...], low, preferred_element_type=F32)
        part_ref[pl.ds(2 * i, SRC * PATCH, stride=HALF), :] = both[:, :PE]
        part_ref[pl.ds(2 * i + 1, SRC * PATCH, stride=HALF), :] = both[:, PE:]
        return carry

    lax.fori_loop(0, HALF // 2, pair, 0, unroll=2)


def start_strips(part_ref, parts, send, recv):
    me, y = lax.axis_index("recv"), lax.axis_index("src")
    rows = PATCH * HALF
    copies = []
    for dy in (2, 1, 3):
        to = (y + dy) % SRC
        copies.append(
            pltpu.make_async_remote_copy(
                src_ref=part_ref.at[pl.ds(to * rows, rows)], dst_ref=parts.at[dy - 1],
                send_sem=send.at[dy - 1], recv_sem=recv.at[dy - 1],
                device_id=(me, to), device_id_type=MESH,
            )
        )
        copies[-1].start()
    return copies


def strip_sum(p, part_ref, parts):
    y = lax.axis_index("src")
    own = part_ref[pl.ds(pl.multiple_of((y * PATCH + p) * HALF, HALF), HALF), :]
    at = pl.ds(pl.multiple_of(p * HALF, HALF), HALF)
    return own + parts[0, at, :] + parts[1, at, :] + parts[2, at, :]


def solve_patch(p, time, count, stress, pre_ref, fri_ref, load_ref):
    pre, fri, load = pre_ref[pl.ds(p, 1), :], fri_ref[pl.ds(p, 1), :], load_ref[pl.ds(p, 1), :]
    times = lax.broadcasted_iota(jnp.int32, (count, PE), 0).astype(F32) + float(time + 1)
    drive = pre + load * times
    if stress is not None:
        drive = drive + stress
    return newton(drive, jnp.broadcast_to(fri, (count, PE)))


PEERS = (4, 3, 5, 2, 6, 7, 1)
CUTS = 2
STEP = 4


def rupture_kernel(
    n_z, inter_ref, inter_rows, length_ref, pre_ref, fri_ref, load_ref, kern_ref, out_ref,
    zbuf, req, wanted_ref, asked, chosen, table_ref, kern_f32, early_ref, got_ref,
    rows, weight, high, low, carry_ref, terms, route_ref, picked, *rest
):
    half, quarter = n_z // 2, n_z // STEP
    part, parts, own, rest = rest[0:4], rest[4:8], rest[8:10], rest[10:]
    right = {s: rest[2 * s - 2 : 2 * s] for s in range(1, half)}
    left = {s: rest[2 * (half + s) - 4 : 2 * (half + s) - 2] for s in range(1, half)}
    far = rest[4 * half - 4 : 4 * half - 2]
    req_s, req_r, z_s, z_r, ask_s, ask_r, y_s, y_r, r_s, r_r, l_s, l_r, x_s, x_r, loc = rest[4 * half - 2 :]
    right[half] = left[half] = far
    right[0] = left[0] = own
    me, y = lax.axis_index("recv"), lax.axis_index("src")
    z, k_me = me // GRP, me % GRP

    def at_z(dz):
        return (((z + dz + n_z) % n_z) * GRP + k_me, y)

    to_right, to_left = at_z(1), at_z(-1)
    barrier = pltpu.get_barrier_semaphore()
    for dy in range(1, SRC):
        pl.semaphore_signal(barrier, inc=1, device_id=(me, (y + dy) % SRC), device_id_type=MESH)
    for dz in (*range(STEP, n_z, STEP), 1, -1, -2):
        pl.semaphore_signal(barrier, inc=1, device_id=at_z(dz), device_id_type=MESH)
    for dk in range(1, GRP):
        pl.semaphore_signal(barrier, inc=1, device_id=(z * GRP + (k_me + dk) % GRP, y), device_id_type=MESH)
    fetch = pltpu.make_async_copy(kern_ref, kern_f32, loc.at[0])
    fetch.start()

    mine_at = (z % STEP) * quarter + z // STEP
    zbuf[mine_at, 0:8, :] = pre_ref[...]
    zbuf[mine_at, 8:16, :] = fri_ref[...]
    zbuf[mine_at, 16:24, :] = load_ref[...]
    row = inter_rows[1:2, :]
    eye = lax.broadcasted_iota(jnp.int32, (NENT, NENT), 0) == lax.broadcasted_iota(jnp.int32, (NENT, NENT), 1)
    column = jnp.sum(jnp.where(eye, jnp.broadcast_to(row, (NENT, NENT)), 0), axis=1, keepdims=True)
    owner_of = lax.shift_right_logical(column, 5)
    place_of = jnp.bitwise_and(column, PATCH - 1)
    hit = owner_of == lax.broadcasted_iota(jnp.int32, (NENT, n_z * GRP), 1)
    wanted = jnp.max(jnp.where(hit, place_of, 0), axis=0, keepdims=True)
    req[k_me] = jnp.broadcast_to(wanted, (8, n_z * GRP))
    route_ref[...] = routes(inter_rows, length_ref[0])

    def clear(k, carry):
        got_ref[k, :, 0:HALF, :] = jnp.zeros((n_z, HALF, PE), F32)
        return carry

    lax.fori_loop(0, GRP, clear, 0)
    pl.semaphore_wait(barrier, SRC - 1 + quarter - 1 + 3 + GRP - 1)

    def params(at, i, to):
        copy = pltpu.make_async_remote_copy(
            src_ref=zbuf.at[at], dst_ref=zbuf.at[at], send_sem=z_s.at[i], recv_sem=z_r.at[i],
            device_id=to, device_id_type=MESH,
        )
        copy.start()
        return copy

    near = [params(pl.ds(mine_at, 1), i - 1, at_z(i * STEP)) for i in sorted(range(1, quarter), key=lambda i: -min(i, quarter - i))]
    sends = []
    for dk in range(1, GRP):
        sends.append(
            pltpu.make_async_remote_copy(
                src_ref=req.at[k_me], dst_ref=req.at[k_me], send_sem=req_s.at[dk - 1], recv_sem=req_r.at[dk - 1],
                device_id=(z * GRP + (k_me + dk) % GRP, y), device_id_type=MESH,
            )
        )
        sends[-1].start()

    def weights(k, carry):
        for lag in range(LAGS):
            up, down = split(kern_f32[k, pl.ds(lag, PE, stride=LAGS), :].T)
            weight[k, lag * PE : (lag + 1) * PE, 0:PE] = up
            weight[k, lag * PE : (lag + 1) * PE, PE : 2 * PE] = down
            pair = lag // 2
            at, side = LAGS * PE + (pair // 2 * 2 + lag % 2) * PE, (pair % 2) * PE
            weight[k, at : at + PE, side : side + PE] = up
        return carry

    for copy in near:
        copy.wait_recv()
    group = pl.ds((z % STEP) * quarter, quarter)
    others = [params(group, quarter - 1 + i, at_z(dz)) for i, dz in enumerate((2, 1, -1))]
    fetch.wait()
    lax.fori_loop(0, KER, weights, 0)
    for copy in sends:
        copy.wait()
    for k in range(GRP):
        wanted_ref[k : k + 1, :] = req[k, 0:1, :]
    fall = pltpu.make_async_copy(wanted_ref, asked, loc.at[1])
    fall.start()
    fall.wait()
    for copy in others:
        copy.wait()
    for copy in near:
        copy.wait_send()

    def choose(k, carry):
        for zz in range(n_z):
            p = asked[k, zz * GRP + k_me]
            for i in range(3):
                chosen[k, i, zz : zz + 1, :] = zbuf[(zz % STEP) * quarter + zz // STEP, pl.ds(8 * i + p, 1), :]
        return carry

    lax.fori_loop(0, GRP, choose, 0)
    xsends = []
    for dk in PEERS:
        k = (k_me + dk) % GRP
        xsends.append(
            pltpu.make_async_remote_copy(
                src_ref=chosen.at[k], dst_ref=table_ref.at[k_me], send_sem=ask_s.at[dk - 1], recv_sem=ask_r.at[dk - 1],
                device_id=(z * GRP + k, y), device_id_type=MESH,
            )
        )
        xsends[-1].start()
    table_ref[k_me] = chosen[k_me]

    def known(p, carry):
        out_ref[p, 0:BLOCK] = solve_patch(p, 0, BLOCK, None, pre_ref, fri_ref, load_ref)
        return carry

    lax.fori_loop(0, PATCH, known, 0)
    for copy in xsends:
        copy.wait()

    for k in range(KER):
        high[k, 0 : PAD * ENT, :] = jnp.zeros((PAD * ENT, 2 * PE), BF16)
        low[k, 0 : PAD * ENT, :] = jnp.zeros((PAD * ENT, 2 * PE), BF16)

        def fill(e, carry):
            owner = lax.shift_right_logical(inter_ref[1, k * ENT + e], 5)
            zz, kk = owner // GRP, owner % GRP
            for i in range(3):
                rows[k, i, pl.ds(e, 1), :] = table_ref[kk, i, pl.ds(zz, 1), :]
            delay = inter_ref[2, k * ENT + e]
            rows[k, 3, pl.ds(e, 1), :] = jnp.full((1, PE), delay, jnp.int32).astype(F32)
            return carry

        lax.fori_loop(0, ENT, fill, 0, unroll=8)
        history = history_of(k, rows)

        def pair(i, before):
            now, after = history(32 + 2 * i), history(33 + 2 * i)
            side = jnp.concatenate([now, after], axis=0)
            put(k, high, low, (PAD + 2 * i) * ENT, side, jnp.concatenate([before, now], axis=0))
            return after

        lax.fori_loop(0, 16, pair, jnp.zeros((ENT, PE), F32))

    strips = []
    for th in range(2):
        for k in range(KER):
            conv(k, th, 14 - PAD, True, high, low, weight, carry_ref, terms)
        route(th, route_ref, terms, part[th])
        strips.append(start_strips(part[th], parts[th], y_s.at[th], y_r.at[th]))

    moves = {}

    def forward(s, th, h):
        for name, bufs, send, recv, to in (("r", right, r_s, r_r, to_right), ("l", left, l_s, l_r, to_left)):
            if s < half or (s == half and (h < CUTS // 2) == (name == "r")):
                at = pl.ds(h * (PATCH // CUTS), PATCH // CUTS)
                moves[name, s, th, h] = pltpu.make_async_remote_copy(
                    src_ref=bufs[s - 1][th].at[at], dst_ref=bufs[s][th].at[at],
                    send_sem=send.at[s - 1, th * CUTS + h], recv_sem=recv.at[s - 1, th * CUTS + h],
                    device_id=to, device_id_type=MESH,
                )
                moves[name, s, th, h].start()

    def pick(origin, slot, buffers):
        for k in range(GRP):
            for th in range(2):
                picked[k, slot, th * HALF : (th + 1) * HALF] = buffers[th][asked[k, origin * GRP + k_me]]

    def to_peers(first, count):
        for dk in PEERS:
            k = (k_me + dk) % GRP
            pltpu.make_async_remote_copy(
                src_ref=picked.at[k, pl.ds(first, count)], dst_ref=got_ref.at[k_me, pl.ds(first, count), pl.ds(HALF, BLOCK)],
                send_sem=x_s.at[dk - 1], recv_sem=x_r.at[dk - 1],
                device_id=(z * GRP + k, y), device_id_type=MESH,
            ).start()

    def early(i):
        def one(k, carry):
            history = history_of(k, rows)
            for b in range(4 * i, 4 * i + 4, 2):
                early_ref[k, b * ENT : (b + 2) * ENT, :] = jnp.concatenate([history(b + 48), history(b + 49)], axis=0)
            return carry

        lax.fori_loop(0, KER, one, 0)

    for th in range(2):
        for copy in strips[th]:
            copy.wait_recv()

        def solve(p, carry):
            v = solve_patch(p, BLOCK + th * HALF, HALF, strip_sum(p, part[th], parts[th]), pre_ref, fri_ref, load_ref)
            own[th][p] = v
            out_ref[p, BLOCK + th * HALF : BLOCK + (th + 1) * HALF] = v
            return carry

        lax.fori_loop(0, PATCH, solve, 0)
        for h in range(CUTS):
            forward(1, th, h)
    def line_up(k, i, carry):
        left = early_ref[k, pl.ds(pl.multiple_of((2 * i + 2) * ENT, 2 * ENT), 2 * ENT), :]
        right = early_ref[k, pl.ds(pl.multiple_of((2 * i + 1) * ENT, ENT), 2 * ENT), :]
        put(k, high, low, 2 * i * ENT, left, right)
        return carry

    pick(z, 0, own)
    to_peers(0, 1)
    for s in range(1, half + 1):
        early(s - 1)
        if s > half - KER:
            k = s - (half - KER) - 1
            early_ref[k, 32 * ENT :, :] = jnp.zeros((16 * ENT, PE), F32)
            lax.fori_loop(0, 7, functools.partial(line_up, k), 0)
        for th in range(2):
            for h in range(CUTS):
                for name in "rl":
                    if (name, s, th, h) in moves:
                        moves[name, s, th, h].wait_recv()
                forward(s + 1, th, h)
        if s < half:
            pick((z + n_z - s) % n_z, 2 * s - 1, right[s])
            pick((z + s) % n_z, 2 * s, left[s])
            to_peers(2 * s - 1, 2)
        else:
            pick((z + half) % n_z, n_z - 1, far)
            to_peers(n_z - 1, 1)
    mine = pltpu.make_async_copy(picked.at[k_me], got_ref.at[k_me, :, pl.ds(HALF, BLOCK)], loc.at[2])
    mine.start()
    for dk in range(1, GRP):
        k = (k_me + dk) % GRP
        pltpu.make_async_remote_copy(
            src_ref=picked.at[k], dst_ref=got_ref.at[k_me, :, pl.ds(HALF, BLOCK)], send_sem=x_s.at[dk - 1], recv_sem=x_r.at[dk - 1],
            device_id=(z * GRP + k, y), device_id_type=MESH,
        ).wait()
    mine.wait()

    for k in range(KER):
        def place(e, carry):
            owner = lax.shift_right_logical(inter_ref[1, k * ENT + e], 5)
            delay = inter_ref[2, k * ENT + e]
            ahead = (owner // GRP - z + n_z) % n_z
            slot = jnp.where(ahead < n_z // 2, 2 * ahead, 2 * (n_z - ahead) - 1)
            early_ref[k, pl.ds(16 * ENT + e, BLOCK, stride=ENT), :] += got_ref[owner % GRP, slot, pl.ds(jnp.clip(48 - delay, 0, HALF), BLOCK), :]
            return carry

        lax.fori_loop(0, ENT, place, 0, unroll=8)

        lax.fori_loop(7, 23, functools.partial(line_up, k), 0)

    for th in range(2):
        for k in range(KER):
            conv(k, th, 0, False, high, low, weight, carry_ref, terms)
        route(th, route_ref, terms, part[2 + th])
        strips.append(start_strips(part[2 + th], parts[2 + th], y_s.at[2 + th], y_r.at[2 + th]))
    for th in range(2):
        for copy in strips[2 + th]:
            copy.wait_recv()

        def solve(p, carry):
            at = pl.ds(2 * BLOCK + th * HALF, HALF)
            stress = strip_sum(p, part[2 + th], parts[2 + th])
            out_ref[p, at] = solve_patch(p, 2 * BLOCK + th * HALF, HALF, stress, pre_ref, fri_ref, load_ref)
            return carry

        lax.fori_loop(0, PATCH, solve, 0)
    for copy in moves.values():
        copy.wait_send()
    for group in strips:
        for copy in group:
            copy.wait_send()


def local(interactions, list_lengths, kernels, prestress, friction, load_rate):
    n_z = lax.axis_size("recv") // GRP
    half = n_z // 2
    owners = n_z * GRP
    vm = pl.BlockSpec(memory_space=pltpu.VMEM)
    sm = pl.BlockSpec(memory_space=pltpu.SMEM)
    dma = pltpu.SemaphoreType.DMA
    part = pltpu.VMEM((SRC * PATCH * HALF, PE), F32)
    parts = pltpu.VMEM((SRC - 1, PATCH * HALF, PE), F32)
    halves = pltpu.VMEM((PATCH, HALF, PE), F32)
    peers = dma((GRP - 1,))
    return pl.pallas_call(
        functools.partial(rupture_kernel, n_z),
        out_shape=jax.ShapeDtypeStruct((PATCH, 3 * BLOCK, PE), F32),
        in_specs=[sm, vm, sm, vm, vm, vm, pl.BlockSpec(memory_space=pl.ANY)],
        out_specs=vm,
        scratch_shapes=[
            pltpu.VMEM((n_z, 24, PE), F32),
            pltpu.VMEM((GRP, 8, owners), jnp.int32),
            pltpu.VMEM((GRP, owners), jnp.int32),
            pltpu.SMEM((GRP, owners), jnp.int32),
            pltpu.VMEM((GRP, 3, n_z, PE), F32),
            pltpu.VMEM((GRP, 3, n_z, PE), F32),
            pltpu.VMEM((KER, LAGS * PE, PE), F32),
            pltpu.VMEM((KER, 48 * ENT, PE), F32),
            pltpu.VMEM((GRP, n_z, HALF + BLOCK, PE), F32),
            pltpu.VMEM((KER, 4, ENT, PE), F32),
            pltpu.VMEM((KER, WIDE, 2 * PE), BF16),
            pltpu.VMEM((KER, 46 * ENT, 2 * PE), BF16),
            pltpu.VMEM((KER, 46 * ENT, 2 * PE), BF16),
            pltpu.VMEM((KER, 2 * ENT, PE), F32),
            pltpu.VMEM((KER, BLOCK * ENT, PE), F32),
            pltpu.VMEM((SRC * PATCH, NENT), BF16),
            pltpu.VMEM((GRP, n_z, BLOCK, PE), F32),
            part, part, part, part, parts, parts, parts, parts,
            *[halves for _ in range(2 + 2 * (2 * (half - 1) + 1))],
            peers, peers, dma((n_z // STEP + 2,)), dma((n_z // STEP + 2,)), peers, peers,
            dma((4, SRC - 1)), dma((4, SRC - 1)),
            *[dma((half, 2 * CUTS)) for _ in range(4)],
            peers, peers, dma((3,)),
        ],
        compiler_params=pltpu.CompilerParams(
            collective_id=0, has_side_effects=True, vmem_limit_bytes=VMEM_LIMIT
        ),
        name="rupture",
    )(interactions, interactions, list_lengths, prestress, friction, load_rate, kernels.reshape(KER, PE * LAGS, PE))


def solution(mesh):
    own = P(("recv", "src"))
    in_specs = (
        P(None, ("recv", "src")),
        own,
        P(("recv", "src"), None, None, None),
        P(("recv", "src"), None),
        P(("recv", "src"), None),
        P(("recv", "src"), None),
    )
    out_specs = P(("recv", "src"), None, None)
    return jax.shard_map(local, mesh=mesh, in_specs=in_specs, out_specs=out_specs, check_vma=False)
```
